32 devices in a mesh: runs: 2 (over y), lon: 4 (over z), tag: 2 (over x), lev: 2 (over core).
Axes of the slice: x: 2, y: 2, z: 4, core: 2. Of those that a mesh axis runs over, the one named last changes fastest.
Arguments:
- tracer: float32 [128, 2, 1152, 768], P(('runs', 'tag'), 'lev', 'lon'), parts along dimension 0, may hold values from -6 to 6
- courant: float32 [2, 4, 1152, 768], P(None, ('runs', 'lev'), ('lon', 'tag')), parts along dimension 1, may hold values from -1 to 1
- thickness: float32 [4, 1152, 768], P(('runs', 'lev'), ('lon', 'tag')), parts along dimension 0, may hold values from 0.5 to 2
- emission: bfloat16 [8, 1152, 768], P(None, 'lon'), may hold values from -6 to 6
- region_map: int32 [128], P(('runs', 'tag')), parts along dimension 0, may hold values from 0 to 7
- filter_mask: int32 [768], replicated, may hold values from 0 to 1, as said below
- cutoff: int32 [768], replicated, may hold values from 16 to 576
Outputs:
- new_tracer: float32 [128, 2, 1152, 768], P(('runs', 'tag'), 'lev', 'lon'), parts along dimension 0
The draws below stay inside these ranges and needn't reach their ends.
There are 2 independent parts, one for each index of `runs`. The reference program is written for one: setup_inputs(seed, part) draws one part's arguments, and reference() takes and returns one part's arrays. A program takes and returns all parts, laid end to end along the dimension named above; an argument that names none is the same for every part. Nothing has to cross between parts.
Inputs may be any that keep to these rules, and one draw needn't show every extreme that they name: `filter_mask`: exactly 128 latitudes carry a 1.
All inputs are finite; a program needn't handle non-finite values.
Results may differ from the reference program's by a relative error of at most 0.0003.
Values sent between devices are 32-bit elements; how exact they have to be, the bound alone decides.
No kernel may reach another device: no remote copies, remote signals or barrier semaphores. Data moves between devices by JAX's collectives and lax.ppermute only.
A program may use at most 448 MiB of HBM per device.

```python
import math
import jax
import jax.numpy as jnp
from jax import lax

LON = 1152
LAT = 768
TAGS = 64
REGIONS = 8
FROWS = 128
LEV = 2


def draw_filter_mask(key, part):
    key = jax.random.fold_in(key, 7)
    ranking = jax.random.permutation(key, LAT)
    return (ranking < FROWS).astype(jnp.int32)


def plant(result, key, least, largest):
    dims = result.shape
    spot = [jax.random.randint(jax.random.fold_in(key, axis), (), 0, dims[axis]) for axis in range(len(dims))]
    result = result.at[tuple(spot)].set(least)
    longest = dims.index(max(dims))
    spot[longest] = (spot[longest] + 1) % dims[longest]
    return result.at[tuple(spot)].set(largest)


def block_levels(own_key, shape, cuts, low, high):
    loudness = 1.0
    for axis_at, blocks in cuts:
        heights = jax.random.uniform(jax.random.fold_in(jax.random.fold_in(own_key, 6), axis_at), (blocks,), jnp.float32, low / len(cuts), high / len(cuts))
        loudness = loudness * jnp.repeat(jnp.exp(heights), shape[axis_at] // blocks).reshape((-1,) + (1,) * (len(shape) - 1 - axis_at))
    return loudness


def gaussian(key, shape, scale, most, shards=(), held_as=jnp.bfloat16):
    loudness = block_levels(key, shape, shards, -0.22, 0.18) if shards else 1.0
    result = jax.random.normal(key, shape, jnp.float32) * scale * loudness
    return jnp.minimum(jnp.maximum(result, -most), most).astype(held_as)


def setup_inputs(seed: int = 0, part: int = 0) -> dict:
    seeds = jax.random.split(jax.random.key(seed), 8)
    part_keys = jax.random.split(jax.random.fold_in(seeds[7], part), 8)
    tracer = gaussian(part_keys[0], (TAGS, LEV, LON, LAT), 1.0, 6.0, ((0, 2), (1, 2), (2, 4)), jnp.float32)
    courant = gaussian(part_keys[1], (2, LEV, LON, LAT), 0.25, 1.0, ((1, 2), (2, 8)), jnp.float32)
    thickness = jnp.clip(jnp.exp(math.log(2.0) - 1.3862944 * jax.random.uniform(part_keys[2], (LEV, LON, LAT), jnp.float32) ** block_levels(part_keys[2], (LEV, LON, LAT), ((0, 2), (1, 8)), -0.2, 0.2)), 0.5, 2.0)
    emission = gaussian(seeds[3], (REGIONS, LON, LAT), 1.0, 6.0, ((1, 4),))
    region_map = plant(jax.random.randint(part_keys[4], (TAGS,), 0, REGIONS), jax.random.fold_in(part_keys[4], 1), 0, REGIONS - 1).astype(jnp.int32)
    filter_mask = draw_filter_mask(jax.random.fold_in(seeds[7], 71), part)
    cutoff = plant(jax.random.randint(seeds[6], (LAT,), 16, LON // 2 + 1), jax.random.fold_in(seeds[6], 1), 16, (LON // 2 + 1) - 1).astype(jnp.int32)
    return dict(tracer=tracer, courant=courant, thickness=thickness, emission=emission, region_map=region_map, filter_mask=filter_mask, cutoff=cutoff)


def face_flux(back_two, back_one, centre, ahead, courant_face):
    edge = (7.0 * (back_one + centre) - (back_two + ahead)) / 12.0
    return courant_face * edge - 0.5 * jnp.abs(courant_face) * (centre - back_one)


def meridional(field, courant_merid):
    lat_count = field.shape[-1]
    widths = [(0, 0)] * (field.ndim - 1) + [(2, 1)]
    padded = jnp.pad(field, widths)
    flux = face_flux(padded[..., 0:lat_count], padded[..., 1:lat_count + 1], field, padded[..., 3:lat_count + 3], courant_merid)
    inside = (jnp.arange(lat_count, dtype=jnp.int32) > 0).astype(field.dtype)
    flux = flux * inside
    closing = jnp.zeros_like(flux[..., :1])
    return jnp.concatenate([flux[..., 1:], closing], axis=-1) - flux


def reference(tracer, courant, thickness, emission, region_map, filter_mask, cutoff):
    zonal = courant[0]
    merid = courant[1]
    wavenumber = jnp.arange(LON // 2 + 1, dtype=jnp.int32)
    keeping = jnp.where(filter_mask[None, :] == 1, wavenumber[:, None] <= cutoff[None, :], True)
    keeping = keeping.astype(tracer.dtype)

    def one_tag(inputs):
        field, region = inputs
        source = jnp.take(emission, region, axis=0).astype(tracer.dtype)
        back_one = jnp.roll(field, 1, axis=1)
        back_two = jnp.roll(field, 2, axis=1)
        ahead = jnp.roll(field, -1, axis=1)
        zonal_flux = face_flux(back_two, back_one, field, ahead, zonal)
        zonal_div = jnp.roll(zonal_flux, -1, axis=1) - zonal_flux
        merid_div = meridional(field, merid)
        tendency = source[None] - (zonal_div + merid_div) / thickness
        spectrum = jnp.fft.rfft(tendency, axis=1)
        filtered = jnp.fft.irfft(spectrum * keeping[None], n=LON, axis=1)
        return field + filtered.astype(field.dtype)

    return lax.map(one_tag, (tracer, region_map))
```

```python
import functools

import jax
import jax.numpy as jnp
import ml_dtypes
import numpy as np
from jax import lax
from jax.experimental import pallas as pl
from jax.experimental.pallas import tpu as pltpu
from jax.sharding import PartitionSpec as P

FROWS = 128
GROUP = 8
WAVES = 32
LANES = 128
CHUNK = 4
CAPS = (0.6, 0.66, 1.0)
VMEM = 24 * 1024 * 1024


def wave_table(length):
    waves = np.arange(length // 4).reshape(-1, WAVES)
    phase = (np.arange(length)[:, None, None] * waves[None]) % length
    angle = phase * (2.0 * np.pi / length)
    table = np.concatenate([np.cos(angle), np.sin(angle)], axis=-1).reshape(length, -1)
    high = table.astype(ml_dtypes.bfloat16)
    low = (table - high.astype(np.float64)).astype(ml_dtypes.bfloat16)
    return high, low


def halves(value):
    high = value.astype(jnp.bfloat16)
    low = (value - high.astype(jnp.float32)).astype(jnp.bfloat16)
    return high, low


def mxu(left, right, contract=((1,), (0,))):
    return lax.dot_general(left, right, (contract, ((), ())), preferred_element_type=jnp.float32)


def divergence(face, next_face):
    half, next_half = 0.5 * jnp.abs(face), 0.5 * jnp.abs(next_face)
    return (
        face / 12.0,
        -next_face / 12.0 - 7.0 / 12.0 * face - half,
        7.0 / 12.0 * (next_face - face) + half + next_half,
        7.0 / 12.0 * next_face - next_half + face / 12.0,
        -next_face / 12.0,
    )


def stencil_weights(zonal, zonal_next, merid, merid_next, factor):
    east = divergence(zonal, zonal_next)
    north = divergence(merid, merid_next)
    parts = [east[0], east[1], east[3], east[4], north[0], north[1], north[3], north[4], east[2] + north[2]]
    return jnp.stack([part * factor for part in parts])


def forward_kernel(
    cap, offset_ref, region_ref, q_ref, edge_ref, weight_ref, source_ref, stays_ref, pick_ref, sign_ref,
    high_ref, low_ref, moved_ref, out_ref, wide, tendency, spectrum, *, first
):
    length, lats = q_ref.shape[1:]
    columns = high_ref.shape[1]
    step = 16
    for s in range(2):
        wide[s, 6:8] = edge_ref[s, 0:2]
        wide[s, 8:24] = q_ref[s, 0:16]
        wide[s, 40:56] = q_ref[s, length - 16 : length]
        wide[s, 56:58] = edge_ref[s, 2:4]
    stays = stays_ref[...]
    regions = [region_ref[first + 2 * pl.program_id(0) + s] for s in range(2)]
    for start in range(0, length, step):
        rows = min(step, length - start)
        here = slice(start, start + rows)
        for s in range(2):
            q = q_ref[s, here]
            total = source_ref[regions[s], here].astype(jnp.float32) + weight_ref[8, here] * q
            for index, shift in enumerate((-2, -1, 1, 2)):
                if start + shift < 0:
                    moved = wide[s, 8 + shift : 8 + shift + rows]
                elif start + rows + shift > length:
                    moved = wide[s, 56 - rows + shift : 56 + shift]
                else:
                    moved = q_ref[s, start + shift : start + shift + rows]
                total += weight_ref[index, here] * moved
                total += weight_ref[4 + index, here] * pltpu.roll(q, (-shift) % lats, 1)
            moved_ref[s, here] = q + stays * total
            tendency[s, here] = total
    for s in range(2):
        t_high, t_low = halves(tendency[s])
        x = (mxu(t_high, pick_ref[...]) + mxu(t_low, pick_ref[...])) * sign_ref[...]
        x_high, x_low = halves(x.T)
        spectrum[s, :, :columns] = (
            mxu(x_high, high_ref[...]) + mxu(x_high, low_ref[...]) + mxu(x_low, high_ref[...])
        )
    left = lax.broadcasted_iota(jnp.int32, (GROUP, LANES), 1) < 2 * WAVES
    for block in range(columns // (2 * WAVES)):
        lanes = slice(LANES * (block // 2), LANES * (block // 2) + LANES)
        for group in range(FROWS // GROUP):
            a = spectrum[0, GROUP * group : GROUP * (group + 1), lanes]
            b = spectrum[1, GROUP * group : GROUP * (group + 1), lanes]
            if block % 2 == 0:
                tile = jnp.where(left, a, pltpu.roll(b, 2 * WAVES, 1))
            else:
                tile = jnp.where(left, pltpu.roll(a, 2 * WAVES, 1), b)
            out_ref[jnp.minimum(offset_ref[block] + group, cap - 1), 0] = tile


def inverse_kernel(
    cap, offset_ref, end_ref, moved_ref, arrived_ref, held_ref, keep_ref, high_ref, low_ref, flip_ref, put_ref, *rest
):
    out_ref, spectrum = rest[-2:]
    columns = high_ref.shape[1]
    left = lax.broadcasted_iota(jnp.int32, (GROUP, LANES), 1) < 2 * WAVES
    end = lax.broadcasted_iota(jnp.int32, (GROUP, LANES), 0) < GROUP * end_ref[0]
    blocks = columns // (2 * WAVES)

    def load(block, group):
        at = jnp.minimum(offset_ref[block] + group, cap - 1)
        return jnp.where(end, arrived_ref[at, 0], held_ref[at, 0])

    for group in range(FROWS // GROUP):
        for pair in range((blocks + 1) // 2):
            even = load(2 * pair, group)
            odd = load(2 * pair + 1, group) if 2 * pair + 1 < blocks else even
            where = slice(GROUP * group, GROUP * (group + 1)), slice(LANES * pair, LANES * (pair + 1))
            keep = keep_ref[where]
            a = jnp.where(left, even, pltpu.roll(odd, 2 * WAVES, 1))
            b = jnp.where(left, pltpu.roll(even, 2 * WAVES, 1), odd)
            spectrum[(0,) + where] = jnp.where(keep != 0.0, a * keep, 0.0)
            spectrum[(1,) + where] = jnp.where(keep != 0.0, b * keep, 0.0)
    for s in range(2):
        s_high, s_low = halves(spectrum[s, :, :columns])
        both = ((1,), (1,))
        back = mxu(high_ref[...], s_high, both) + mxu(high_ref[...], s_low, both) + mxu(low_ref[...], s_high, both)
        b_high, b_low = halves(back * flip_ref[...])
        out_ref[s] = moved_ref[s] + (mxu(b_high, put_ref[...]) + mxu(b_low, put_ref[...]))


RESIDENT = pl.BlockSpec(memory_space=pltpu.VMEM)


def forward(chunk, cap, offsets, regions, tracer, edges, weights, source, stays, pick, sign, high, low):
    tags, length, lats = tracer.shape
    pairs = CHUNK // 2
    base = chunk * pairs
    constants = [weights, source, stays, pick, sign, high, low]
    grid_spec = pltpu.PrefetchScalarGridSpec(
        num_scalar_prefetch=2,
        grid=(pairs,),
        in_specs=[
            pl.BlockSpec((2, length, lats), lambda p, *_: (base + p, 0, 0)),
            pl.BlockSpec((2, 4, lats), lambda p, *_: (base + p, 0, 0)),
        ]
        + [RESIDENT] * len(constants),
        out_specs=[
            pl.BlockSpec((2, length, lats), lambda p, *_: (p, 0, 0)),
            pl.BlockSpec((cap, 1, GROUP, LANES), lambda p, *_: (0, p, 0, 0)),
        ],
        scratch_shapes=[
            pltpu.VMEM((2, 64, lats), jnp.float32),
            pltpu.VMEM((2, length, lats), jnp.float32),
            pltpu.VMEM((2, FROWS, -(-high.shape[1] // LANES) * LANES), jnp.float32),
        ],
    )
    flops = CHUNK * 2 * length * (2 * lats * FROWS + 3 * high.shape[1] * FROWS)
    return pl.pallas_call(
        functools.partial(forward_kernel, cap, first=chunk * CHUNK),
        grid_spec=grid_spec,
        out_shape=[
            jax.ShapeDtypeStruct((CHUNK, length, lats), jnp.float32),
            jax.ShapeDtypeStruct((cap, pairs, GROUP, LANES), jnp.float32),
        ],
        compiler_params=pltpu.CompilerParams(vmem_limit_bytes=VMEM),
        cost_estimate=pl.CostEstimate(flops=flops, bytes_accessed=5 * CHUNK * length * lats * 4, transcendentals=0),
        name="step_and_transform",
    )(offsets, regions, tracer, edges, *constants)


def inverse(chunk, cap, offsets, end, tracer, moved, arrived, held, keep, high, low, flip, put, out):
    tags, length, lats = tracer.shape
    pairs = CHUNK // 2
    base = chunk * pairs
    constants = [keep, high, low, flip, put]
    specs = [
        pl.BlockSpec((2, length, lats), lambda p, *_: (p, 0, 0)),
        pl.BlockSpec((cap, 1, GROUP, LANES), lambda p, *_: (0, p, 0, 0)),
        pl.BlockSpec((cap, 1, GROUP, LANES), lambda p, *_: (0, p, 0, 0)),
    ] + [RESIDENT] * len(constants)
    operands = [offsets, end, moved, arrived, held] + constants
    aliases = {}
    if out is not None:
        specs.append(pl.BlockSpec(memory_space=pl.ANY))
        operands.append(out)
        aliases = {len(operands) - 1: 0}
    grid_spec = pltpu.PrefetchScalarGridSpec(
        num_scalar_prefetch=2,
        grid=(pairs,),
        in_specs=specs,
        out_specs=pl.BlockSpec((2, length, lats), lambda p, *_: (base + p, 0, 0)),
        scratch_shapes=[pltpu.VMEM((2, FROWS, keep.shape[1]), jnp.float32)],
    )
    flops = CHUNK * 2 * length * (2 * lats * FROWS + 3 * high.shape[1] * FROWS)
    return pl.pallas_call(
        functools.partial(inverse_kernel, cap),
        grid_spec=grid_spec,
        out_shape=jax.ShapeDtypeStruct(tracer.shape, jnp.float32),
        input_output_aliases=aliases,
        compiler_params=pltpu.CompilerParams(vmem_limit_bytes=VMEM),
        cost_estimate=pl.CostEstimate(flops=flops, bytes_accessed=2 * CHUNK * length * lats * 4, transcendentals=0),
        name="restore",
    )(*operands)


def sum_over_lon(packed, count, place):
    middle = count // 2
    total = packed
    for hop in range(middle - 1):
        inward = [(hop, hop + 1), (count - 1 - hop, count - 2 - hop)]
        total = total + lax.ppermute(total, "lon", inward)
    total = total + lax.ppermute(total, "lon", [(middle - 1, middle), (middle, middle - 1)])
    for hop in range(middle - 2, -1, -1):
        outward = [(hop + 1, hop), (count - 2 - hop, count - 1 - hop)]
        arrived = lax.ppermute(total, "lon", outward)
        total = jnp.where((place == hop) | (place == count - 1 - hop), arrived, total)
    return total


def plain_pipeline(chunks, forward_at, inverse_at, place, count, offsets):
    out = None
    for chunk in range(chunks):
        moved, packed = forward_at(chunk, offsets)
        total = sum_over_lon(packed, count, place)
        out = inverse_at(chunk, moved, total, total, out, offsets)
    return out


def stepped_pipeline(chunks, forward_at, inverse_at, place, count, offsets):
    swap = [(0, 1), (1, 0), (2, 3), (3, 2)]
    cross = [(1, 2), (2, 1)]
    end = (place == 0) | (place == count - 1)
    moved, own = {}, {}
    moved[0], own[0] = forward_at(0, offsets)
    pair_sum = swapped = crossed = sent = out = None
    for t in range(chunks + 3):
        arrived, held = swapped, sent
        total = None if crossed is None else pair_sum + crossed
        here = own.get(t)
        if here is None:
            sent = total
        else:
            sent = here if total is None else jnp.where(end, here, total)
        pair_sum = own[t - 1] + swapped if 1 <= t <= chunks else None
        if t < chunks + 2:
            sending = [x for x in (sent, pair_sum) if x is not None]
            extra = [out] if out is not None else []
            result = lax.optimization_barrier((offsets, *sending, *extra))
            token, result = result[0], list(result[1:])
            if sent is not None:
                sent = result.pop(0)
            if pair_sum is not None:
                pair_sum = result.pop(0)
            if extra:
                out = result.pop(0)
            swapped = None if sent is None else lax.ppermute(sent, "lon", swap)
            crossed = None if pair_sum is None else lax.ppermute(pair_sum, "lon", cross)
        else:
            token = offsets
        if t + 1 < chunks:
            moved[t + 1], own[t + 1] = forward_at(t + 1, token)
        if t >= 3:
            out = inverse_at(t - 3, moved[t - 3], arrived, held, out, token)
    return out


def ring_edges(first, last, count):
    forward_ring = [(i, (i + 1) % count) for i in range(count)]
    backward_ring = [((i + 1) % count, i) for i in range(count)]
    before = lax.ppermute(last, "lon", forward_ring)
    after = lax.ppermute(first, "lon", backward_ring)
    return before, after


def body(tracer, courant, thickness, emission, region_map, filter_mask, cutoff):
    tracer = tracer[:, 0]
    courant, thickness = courant[:, 0], thickness[0]
    tags, length, lats = tracer.shape
    count = lax.axis_size("lon")
    place = lax.axis_index("lon")
    full = length * count
    nyquist = full // 2
    groups = FROWS // GROUP
    backward_ring = [((i + 1) % count, i) for i in range(count)]

    flipped = cutoff > nyquist - 1 - cutoff
    reach = jnp.minimum(cutoff, nyquist - 1 - cutoff)
    masked = filter_mask == 1
    score = jnp.where(masked, reach + 2, 0)
    lat = jnp.arange(lats, dtype=jnp.int32)
    ahead = (score[None, :] > score[:, None]) | ((score[None, :] == score[:, None]) & (lat[None, :] < lat[:, None]))
    rank = jnp.sum(ahead.astype(jnp.int32), axis=1)
    chosen = rank[:, None] == jnp.arange(FROWS, dtype=jnp.int32)[None, :]
    row_reach = jnp.sum(jnp.where(chosen, reach[:, None], 0), axis=0)
    row_flipped = jnp.any(chosen & flipped[:, None], axis=0)
    one_hot = chosen.astype(jnp.bfloat16)
    put = one_hot.T

    blocks = nyquist // 2 // WAVES
    starts = jnp.arange(blocks, dtype=jnp.int32) * WAVES
    needed = jnp.sum((row_reach[None, :] >= starts[:, None]).astype(jnp.int32), axis=1)
    sizes = (needed + GROUP - 1) // GROUP
    offsets = jnp.sum(
        jnp.where(jnp.arange(blocks)[None, :] < jnp.arange(blocks)[:, None], sizes[None, :], 0), axis=1
    ).astype(jnp.int32)
    used = jnp.sum(sizes)

    lane = jnp.arange(-(-blocks * 2 * WAVES // LANES) * LANES, dtype=jnp.int32)
    wave = lane // (2 * WAVES) * WAVES + lane % WAVES
    scaling = jnp.where(wave == 0, 1.0 / full, 2.0 / full).astype(jnp.float32)
    keep = jnp.where(wave[None, :] <= row_reach[:, None], scaling[None, :], 0.0)
    high, low = (
        lax.dynamic_slice_in_dim(jnp.asarray(table), place * length, length, 0) for table in wave_table(full)
    )
    odd = (place * length + jnp.arange(length, dtype=jnp.int32)) % 2 == 1
    sign = jnp.where(odd[:, None] & row_flipped[None, :], -1.0, 1.0).astype(jnp.float32)
    flip = jnp.where(row_flipped[None, :], -sign, sign)
    stays = jnp.where(masked & ~flipped, 0.0, 1.0).astype(jnp.float32)[None, :]

    largest = blocks * groups

    def run(cap):
        zonal, merid = courant[0], courant[1] * (lat > 0).astype(jnp.float32)
        fields = lax.all_gather(jnp.concatenate([zonal[None], merid[None], thickness[None]]), "tag", axis=1, tiled=True)
        zonal_after = jnp.concatenate([fields[0, 1:], lax.ppermute(fields[0, :1], "lon", backward_ring)])
        merid_after = jnp.pad(fields[1, :, 1:], ((0, 0), (0, 1)))
        weights = stencil_weights(fields[0], zonal_after, fields[1], merid_after, -1.0 / fields[2])
        ones = jnp.ones_like(lat, dtype=bool)
        inside = jnp.stack([ones] * 4 + [lat >= 2, lat >= 1, lat <= lats - 2, lat <= lats - 3] + [ones])
        weights = weights * inside.astype(jnp.float32)[:, None, :]
        edges = jnp.concatenate(ring_edges(tracer[:, :2], tracer[:, length - 2 :], count), axis=1)
        is_end = ((place == 0) | (place == count - 1)).astype(jnp.int32).reshape(1)

        def forward_at(chunk, offsets):
            return forward(
                chunk, cap, offsets, region_map, tracer, edges, weights, emission, stays, one_hot, sign, high, low
            )

        def inverse_at(chunk, moved, arrived, held, out, offsets):
            return inverse(chunk, cap, offsets, is_end, tracer, moved, arrived, held, keep, high, low, flip, put, out)

        pipeline = stepped_pipeline if count == 4 else plain_pipeline
        return pipeline(tags // CHUNK, forward_at, inverse_at, place, count, offsets)

    caps = [int(share * largest) + 1 for share in CAPS]
    if len(caps) == 1:
        out = run(caps[0])
    else:
        index = sum((used >= cap).astype(jnp.int32) for cap in caps[:-1])
        out = lax.switch(index, [functools.partial(run, cap) for cap in caps])
    return out[:, None]


def solution(mesh):
    in_specs = (
        P(("runs", "tag"), "lev", "lon", None),
        P(None, ("runs", "lev"), ("lon", "tag"), None),
        P(("runs", "lev"), ("lon", "tag"), None),
        P(None, "lon", None),
        P(("runs", "tag")),
        P(),
        P(),
    )
    out_specs = P(("runs", "tag"), "lev", "lon", None)
    return jax.shard_map(body, mesh=mesh, in_specs=in_specs, out_specs=out_specs, check_vma=False)
```

```python
import functools

import jax
import jax.numpy as jnp
import ml_dtypes
import numpy as np
from jax import lax
from jax.experimental import pallas as pl
from jax.experimental.pallas import tpu as pltpu
from jax.sharding import PartitionSpec as P

FROWS = 128
GROUP = 8
WAVES = 32
LANES = 128
CHUNK = 4
CAPS = (0.6, 0.66, 1.0)
VMEM = 24 * 1024 * 1024


def wave_table(length):
    waves = np.arange(length // 4).reshape(-1, WAVES)
    phase = (np.arange(length)[:, None, None] * waves[None]) % length
    angle = phase * (2.0 * np.pi / length)
    table = np.concatenate([np.cos(angle), np.sin(angle)], axis=-1).reshape(length, -1)
    high = table.astype(ml_dtypes.bfloat16)
    low = (table - high.astype(np.float64)).astype(ml_dtypes.bfloat16)
    return high, low


def halves(value):
    high = value.astype(jnp.bfloat16)
    low = (value - high.astype(jnp.float32)).astype(jnp.bfloat16)
    return high, low


def mxu(left, right, contract=((1,), (0,))):
    return lax.dot_general(left, right, (contract, ((), ())), preferred_element_type=jnp.float32)


def divergence(face, next_face):
    half, next_half = 0.5 * jnp.abs(face), 0.5 * jnp.abs(next_face)
    return (
        face / 12.0,
        -next_face / 12.0 - 7.0 / 12.0 * face - half,
        7.0 / 12.0 * (next_face - face) + half + next_half,
        7.0 / 12.0 * next_face - next_half + face / 12.0,
        -next_face / 12.0,
    )


def stencil_weights(zonal, zonal_next, merid, merid_next, factor):
    east = divergence(zonal, zonal_next)
    north = divergence(merid, merid_next)
    parts = [east[0], east[1], east[3], east[4], north[0], north[1], north[3], north[4], east[2] + north[2]]
    return jnp.stack([part * factor for part in parts])


def forward_kernel(
    cap, offset_ref, region_ref, q_ref, edge_ref, weight_ref, source_ref, stays_ref, pick_ref, sign_ref,
    high_ref, low_ref, moved_ref, out_ref, wide, tendency, spectrum, *, first
):
    length, lats = q_ref.shape[1:]
    columns = high_ref.shape[1]
    step = 16
    padded = -(-length // step) * step
    for s in range(2):
        wide[s, 6:8] = edge_ref[s, 0:2]
        wide[s, 8:24] = q_ref[s, 0:16]
        wide[s, 40:56] = q_ref[s, length - 16 : length]
        wide[s, 56:58] = edge_ref[s, 2:4]
    stays = stays_ref[...]
    regions = [region_ref[first + 2 * pl.program_id(0) + s] for s in range(2)]
    for start in range(0, length, step):
        rows = min(step, length - start)
        here = slice(start, start + rows)
        for s in range(2):
            q = q_ref[s, here]
            total = source_ref[regions[s], here].astype(jnp.float32) + weight_ref[8, here] * q
            for index, shift in enumerate((-2, -1, 1, 2)):
                if start + shift < 0:
                    moved = wide[s, 8 + shift : 8 + shift + rows]
                elif start + rows + shift > length:
                    moved = wide[s, 56 - rows + shift : 56 + shift]
                else:
                    moved = q_ref[s, start + shift : start + shift + rows]
                total += weight_ref[index, here] * moved
                total += weight_ref[4 + index, here] * pltpu.roll(q, (-shift) % lats, 1)
            moved_ref[s, here] = q + stays * total
            high, low = halves(total)
            tendency[2 * s * padded + start : 2 * s * padded + start + rows] = high
            tendency[(2 * s + 1) * padded + start : (2 * s + 1) * padded + start + rows] = low
    selected = mxu(tendency[...], pick_ref[...])
    turned = []
    for s in range(2):
        at = 2 * s * padded
        x = (selected[at : at + length] + selected[at + padded : at + padded + length]) * sign_ref[...]
        turned.append(x.T)
    x_high, x_low = halves(jnp.concatenate(turned, axis=0))
    with_high = mxu(jnp.concatenate([x_high, x_low], axis=0), high_ref[...])
    spectrum[:, :columns] = with_high[: 2 * FROWS] + with_high[2 * FROWS :] + mxu(x_high, low_ref[...])
    left = lax.broadcasted_iota(jnp.int32, (GROUP, LANES), 1) < 2 * WAVES
    for block in range(columns // (2 * WAVES)):
        lanes = slice(LANES * (block // 2), LANES * (block // 2) + LANES)
        for group in range(FROWS // GROUP):
            a = spectrum[GROUP * group : GROUP * (group + 1), lanes]
            b = spectrum[FROWS + GROUP * group : FROWS + GROUP * (group + 1), lanes]
            if block % 2 == 0:
                tile = jnp.where(left, a, pltpu.roll(b, 2 * WAVES, 1))
            else:
                tile = jnp.where(left, pltpu.roll(a, 2 * WAVES, 1), b)
            out_ref[jnp.minimum(offset_ref[block] + group, cap - 1), 0] = tile


def inverse_kernel(
    cap, offset_ref, end_ref, moved_ref, arrived_ref, held_ref, keep_ref, high_ref, both_ref, flip_ref, put_ref, *rest
):
    out_ref, spectrum = rest[-2:]
    columns = high_ref.shape[1]
    left = lax.broadcasted_iota(jnp.int32, (GROUP, LANES), 1) < 2 * WAVES
    end = lax.broadcasted_iota(jnp.int32, (GROUP, LANES), 0) < GROUP * end_ref[0]
    blocks = columns // (2 * WAVES)

    def load(block, group):
        at = jnp.minimum(offset_ref[block] + group, cap - 1)
        return jnp.where(end, arrived_ref[at, 0], held_ref[at, 0])

    for group in range(FROWS // GROUP):
        for pair in range((blocks + 1) // 2):
            even = load(2 * pair, group)
            odd = load(2 * pair + 1, group) if 2 * pair + 1 < blocks else even
            where = slice(GROUP * group, GROUP * (group + 1)), slice(LANES * pair, LANES * (pair + 1))
            keep = keep_ref[where]
            a = jnp.where(left, even, pltpu.roll(odd, 2 * WAVES, 1))
            b = jnp.where(left, pltpu.roll(even, 2 * WAVES, 1), odd)
            spectrum[(0,) + where] = jnp.where(keep != 0.0, a * keep, 0.0)
            spectrum[(1,) + where] = jnp.where(keep != 0.0, b * keep, 0.0)
    length = high_ref.shape[0]
    s_high, s_low = halves(spectrum[...].reshape(2 * FROWS, -1)[:, :columns])
    last = ((1,), (1,))
    with_high = mxu(both_ref[...], s_high, last)
    back = with_high[:length] + with_high[length:] + mxu(high_ref[...], s_low, last)
    for s in range(2):
        pieces = jnp.concatenate(halves(back[:, s * FROWS : (s + 1) * FROWS] * flip_ref[...]), axis=1)
        out_ref[s] = moved_ref[s] + mxu(pieces, put_ref[...])


RESIDENT = pl.BlockSpec(memory_space=pltpu.VMEM)


def forward(base, size, cap, offsets, regions, tracer, edges, weights, source, stays, pick, sign, high, low):
    tags, length, lats = tracer.shape
    pairs = size // 2
    constants = [weights, source, stays, pick, sign, high, low]
    grid_spec = pltpu.PrefetchScalarGridSpec(
        num_scalar_prefetch=2,
        grid=(pairs,),
        in_specs=[
            pl.BlockSpec((2, length, lats), lambda p, *_: (base // 2 + p, 0, 0)),
            pl.BlockSpec((2, 4, lats), lambda p, *_: (base // 2 + p, 0, 0)),
        ]
        + [RESIDENT] * len(constants),
        out_specs=[
            pl.BlockSpec((2, length, lats), lambda p, *_: (p, 0, 0)),
            pl.BlockSpec((cap, 1, GROUP, LANES), lambda p, *_: (0, p, 0, 0)),
        ],
        scratch_shapes=[
            pltpu.VMEM((2, 64, lats), jnp.float32),
            pltpu.VMEM((4 * (-(-length // 16) * 16), lats), jnp.bfloat16),
            pltpu.VMEM((2 * FROWS, -(-high.shape[1] // LANES) * LANES), jnp.float32),
        ],
    )
    flops = size * 2 * length * (2 * lats * FROWS + 3 * high.shape[1] * FROWS)
    return pl.pallas_call(
        functools.partial(forward_kernel, cap, first=base),
        grid_spec=grid_spec,
        out_shape=[
            jax.ShapeDtypeStruct((size, length, lats), jnp.float32),
            jax.ShapeDtypeStruct((cap, pairs, GROUP, LANES), jnp.float32),
        ],
        compiler_params=pltpu.CompilerParams(vmem_limit_bytes=VMEM),
        cost_estimate=pl.CostEstimate(flops=flops, bytes_accessed=5 * size * length * lats * 4, transcendentals=0),
        name="step_and_transform",
    )(offsets, regions, tracer, edges, *constants)


def inverse(base, size, cap, offsets, end, tracer, moved, arrived, held, keep, high, both, flip, put, out):
    tags, length, lats = tracer.shape
    pairs = size // 2
    constants = [keep, high, both, flip, put]
    specs = [
        pl.BlockSpec((2, length, lats), lambda p, *_: (p, 0, 0)),
        pl.BlockSpec((cap, 1, GROUP, LANES), lambda p, *_: (0, p, 0, 0)),
        pl.BlockSpec((cap, 1, GROUP, LANES), lambda p, *_: (0, p, 0, 0)),
    ] + [RESIDENT] * len(constants)
    operands = [offsets, end, moved, arrived, held] + constants
    aliases = {}
    if out is not None:
        specs.append(pl.BlockSpec(memory_space=pl.ANY))
        operands.append(out)
        aliases = {len(operands) - 1: 0}
    grid_spec = pltpu.PrefetchScalarGridSpec(
        num_scalar_prefetch=2,
        grid=(pairs,),
        in_specs=specs,
        out_specs=pl.BlockSpec((2, length, lats), lambda p, *_: (base // 2 + p, 0, 0)),
        scratch_shapes=[pltpu.VMEM((2, FROWS, keep.shape[1]), jnp.float32)],
    )
    flops = size * 2 * length * (2 * lats * FROWS + 3 * high.shape[1] * FROWS)
    return pl.pallas_call(
        functools.partial(inverse_kernel, cap),
        grid_spec=grid_spec,
        out_shape=jax.ShapeDtypeStruct(tracer.shape, jnp.float32),
        input_output_aliases=aliases,
        compiler_params=pltpu.CompilerParams(vmem_limit_bytes=VMEM),
        cost_estimate=pl.CostEstimate(flops=flops, bytes_accessed=2 * size * length * lats * 4, transcendentals=0),
        name="restore",
    )(*operands)


def sum_over_lon(packed, count, place):
    middle = count // 2
    total = packed
    for hop in range(middle - 1):
        inward = [(hop, hop + 1), (count - 1 - hop, count - 2 - hop)]
        total = total + lax.ppermute(total, "lon", inward)
    total = total + lax.ppermute(total, "lon", [(middle - 1, middle), (middle, middle - 1)])
    for hop in range(middle - 2, -1, -1):
        outward = [(hop + 1, hop), (count - 2 - hop, count - 1 - hop)]
        arrived = lax.ppermute(total, "lon", outward)
        total = jnp.where((place == hop) | (place == count - 1 - hop), arrived, total)
    return total


def plain_pipeline(chunks, forward_at, inverse_at, place, count, offsets):
    out = None
    for chunk in range(chunks):
        moved, packed = forward_at(chunk, offsets)
        total = sum_over_lon(packed, count, place)
        out = inverse_at(chunk, moved, total, total, out, offsets)
    return out


def stepped_pipeline(chunks, forward_at, inverse_at, place, count, offsets):
    swap = [(0, 1), (1, 0), (2, 3), (3, 2)]
    cross = [(1, 2), (2, 1)]
    end = (place == 0) | (place == count - 1)
    moved, own = {}, {}
    moved[0], own[0] = forward_at(0, offsets)
    pair_sum = swapped = crossed = sent = out = None
    for t in range(chunks + 3):
        arrived, held = swapped, sent
        total = None if crossed is None else pair_sum + crossed
        here = own.get(t)
        if here is None:
            sent = total
        else:
            sent = here if total is None else jnp.where(end, here, total)
        pair_sum = own[t - 1] + swapped if 1 <= t <= chunks else None
        if t < chunks + 2:
            sending = [x for x in (sent, pair_sum) if x is not None]
            extra = [out] if out is not None else []
            result = lax.optimization_barrier((offsets, *sending, *extra))
            token, result = result[0], list(result[1:])
            if sent is not None:
                sent = result.pop(0)
            if pair_sum is not None:
                pair_sum = result.pop(0)
            if extra:
                out = result.pop(0)
            swapped = None if sent is None else lax.ppermute(sent, "lon", swap)
            crossed = None if pair_sum is None else lax.ppermute(pair_sum, "lon", cross)
        else:
            token = offsets
        if t + 1 < chunks:
            moved[t + 1], own[t + 1] = forward_at(t + 1, token)
        if t >= 3:
            out = inverse_at(t - 3, moved[t - 3], arrived, held, out, token)
    return out


def ring_edges(first, last, count):
    forward_ring = [(i, (i + 1) % count) for i in range(count)]
    backward_ring = [((i + 1) % count, i) for i in range(count)]
    before = lax.ppermute(last, "lon", forward_ring)
    after = lax.ppermute(first, "lon", backward_ring)
    return before, after


def body(tracer, courant, thickness, emission, region_map, filter_mask, cutoff):
    tracer = tracer[:, 0]
    courant, thickness = courant[:, 0], thickness[0]
    tags, length, lats = tracer.shape
    count = lax.axis_size("lon")
    place = lax.axis_index("lon")
    full = length * count
    nyquist = full // 2
    groups = FROWS // GROUP
    backward_ring = [((i + 1) % count, i) for i in range(count)]

    flipped = cutoff > nyquist - 1 - cutoff
    reach = jnp.minimum(cutoff, nyquist - 1 - cutoff)
    masked = filter_mask == 1
    score = jnp.where(masked, reach + 2, 0)
    lat = jnp.arange(lats, dtype=jnp.int32)
    ahead = (score[None, :] > score[:, None]) | ((score[None, :] == score[:, None]) & (lat[None, :] < lat[:, None]))
    rank = jnp.sum(ahead.astype(jnp.int32), axis=1)
    chosen = rank[:, None] == jnp.arange(FROWS, dtype=jnp.int32)[None, :]
    row_reach = jnp.sum(jnp.where(chosen, reach[:, None], 0), axis=0)
    row_flipped = jnp.any(chosen & flipped[:, None], axis=0)
    one_hot = chosen.astype(jnp.bfloat16)
    put = one_hot.T

    blocks = nyquist // 2 // WAVES
    starts = jnp.arange(blocks, dtype=jnp.int32) * WAVES
    needed = jnp.sum((row_reach[None, :] >= starts[:, None]).astype(jnp.int32), axis=1)
    taken = (needed + GROUP - 1) // GROUP
    offsets = jnp.sum(
        jnp.where(jnp.arange(blocks)[None, :] < jnp.arange(blocks)[:, None], taken[None, :], 0), axis=1
    ).astype(jnp.int32)
    used = jnp.sum(taken)

    lane = jnp.arange(-(-blocks * 2 * WAVES // LANES) * LANES, dtype=jnp.int32)
    wave = lane // (2 * WAVES) * WAVES + lane % WAVES
    scaling = jnp.where(wave == 0, 1.0 / full, 2.0 / full).astype(jnp.float32)
    keep = jnp.where(wave[None, :] <= row_reach[:, None], scaling[None, :], 0.0)
    high, low = (
        lax.dynamic_slice_in_dim(jnp.asarray(table), place * length, length, 0) for table in wave_table(full)
    )
    odd = (place * length + jnp.arange(length, dtype=jnp.int32)) % 2 == 1
    sign = jnp.where(odd[:, None] & row_flipped[None, :], -1.0, 1.0).astype(jnp.float32)
    flip = jnp.where(row_flipped[None, :], -sign, sign)
    stays = jnp.where(masked & ~flipped, 0.0, 1.0).astype(jnp.float32)[None, :]

    largest = blocks * groups
    both = jnp.concatenate([high, low])
    put = jnp.concatenate([put, put])
    is_end = ((place == 0) | (place == count - 1)).astype(jnp.int32).reshape(1)
    sizes = [CHUNK // 2] + [CHUNK] * ((tags - CHUNK) // CHUNK) + [CHUNK // 2]
    bases = [sum(sizes[:i]) for i in range(len(sizes))]

    gathered = lax.all_gather(courant, "tag", axis=1, tiled=True)
    thick = lax.all_gather(thickness, "tag", axis=0, tiled=True)
    zonal_end = lax.all_gather(lax.ppermute(courant[0, :1], "lon", backward_ring), "tag")[0]
    edges = jnp.concatenate(ring_edges(tracer[:, :2], tracer[:, length - 2 :], count), axis=1)

    def run(cap):
        zonal, merid = gathered[0], gathered[1] * (lat > 0).astype(jnp.float32)
        zonal_after = jnp.concatenate([zonal[1:], zonal_end])
        merid_after = jnp.pad(merid[:, 1:], ((0, 0), (0, 1)))
        weights = stencil_weights(zonal, zonal_after, merid, merid_after, -1.0 / thick)
        ones = jnp.ones_like(lat, dtype=bool)
        inside = jnp.stack([ones] * 4 + [lat >= 2, lat >= 1, lat <= lats - 2, lat <= lats - 3] + [ones])
        weights = weights * inside.astype(jnp.float32)[:, None, :]

        def forward_at(chunk, offsets):
            return forward(
                bases[chunk], sizes[chunk], cap, offsets, region_map, tracer, edges, weights, emission, stays, one_hot,
                sign, high, low,
            )

        def inverse_at(chunk, moved, arrived, held, out, offsets):
            return inverse(
                bases[chunk], sizes[chunk], cap, offsets, is_end, tracer, moved, arrived, held, keep, high, both, flip,
                put, out,
            )

        pipeline = stepped_pipeline if count == 4 else plain_pipeline
        return pipeline(len(sizes), forward_at, inverse_at, place, count, offsets)

    caps = [int(share * largest) + 1 for share in CAPS]
    if len(caps) == 1:
        out = run(caps[0])
    else:
        index = sum((used >= cap).astype(jnp.int32) for cap in caps[:-1])
        out = lax.switch(index, [functools.partial(run, cap) for cap in caps])
    return out[:, None]


def solution(mesh):
    in_specs = (
        P(("runs", "tag"), "lev", "lon", None),
        P(None, ("runs", "lev"), ("lon", "tag"), None),
        P(("runs", "lev"), ("lon", "tag"), None),
        P(None, "lon", None),
        P(("runs", "tag")),
        P(),
        P(),
    )
    out_specs = P(("runs", "tag"), "lev", "lon", None)
    return jax.shard_map(body, mesh=mesh, in_specs=in_specs, out_specs=out_specs, check_vma=False)
```

```python
import functools

import jax
import jax.numpy as jnp
import ml_dtypes
import numpy as np
from jax import lax
from jax.experimental import pallas as pl
from jax.experimental.pallas import tpu as pltpu
from jax.sharding import PartitionSpec as P

FROWS = 128
GROUP = 8
WAVES = 32
LANES = 128
CHUNK = 4
CAPS = (0.605, 0.66, 1.0)
VMEM = 18 * 1024 * 1024


def wave_table(length):
    waves = np.arange(length // 4).reshape(-1, WAVES)
    phase = (np.arange(length)[:, None, None] * waves[None]) % length
    angle = phase * (2.0 * np.pi / length)
    table = np.concatenate([np.cos(angle), np.sin(angle)], axis=-1).reshape(length, -1)
    high = table.astype(ml_dtypes.bfloat16)
    low = (table - high.astype(np.float64)).astype(ml_dtypes.bfloat16)
    return high, low


def halves(value):
    high = value.astype(jnp.bfloat16)
    low = (value - high.astype(jnp.float32)).astype(jnp.bfloat16)
    return high, low


def mxu(left, right, contract=((1,), (0,))):
    return lax.dot_general(left, right, (contract, ((), ())), preferred_element_type=jnp.float32)


def divergence(face, next_face):
    half, next_half = 0.5 * jnp.abs(face), 0.5 * jnp.abs(next_face)
    return (
        face / 12.0,
        -next_face / 12.0 - 7.0 / 12.0 * face - half,
        7.0 / 12.0 * (next_face - face) + half + next_half,
        7.0 / 12.0 * next_face - next_half + face / 12.0,
        -next_face / 12.0,
    )


def weight_kernel(fields_ref, thick_ref, end_ref, out_ref, wide):
    length, lats = thick_ref.shape
    wide[0:length] = fields_ref[0]
    wide[length : length + 1] = end_ref[...]
    lat = lax.broadcasted_iota(jnp.int32, (8, lats), 1)
    for start in range(0, length, 8):
        here = slice(start, start + 8)
        merid = jnp.where(lat > 0, fields_ref[1, here], 0.0)
        north = jnp.where(lat < lats - 1, pltpu.roll(merid, lats - 1, 1), 0.0)
        factor = -1.0 / thick_ref[here]
        along = divergence(wide[here], wide[start + 1 : start + 9])
        across = divergence(merid, north)
        for index, part in enumerate((along[0], along[1], along[3], along[4])):
            out_ref[index, here] = part * factor
        inside = (lat >= 2, lat >= 1, lat <= lats - 2, lat <= lats - 3)
        for index, part in enumerate((across[0], across[1], across[3], across[4])):
            out_ref[4 + index, here] = jnp.where(inside[index], part * factor, 0.0)
        out_ref[8, here] = (along[2] + across[2]) * factor


def stencil_weights(fields, thick, zonal_end):
    length, lats = thick.shape
    return pl.pallas_call(
        weight_kernel,
        in_specs=[RESIDENT] * 3,
        out_specs=RESIDENT,
        out_shape=jax.ShapeDtypeStruct((9, length, lats), jnp.float32),
        scratch_shapes=[pltpu.VMEM((length + 8, lats), jnp.float32)],
        compiler_params=pltpu.CompilerParams(vmem_limit_bytes=VMEM),
        cost_estimate=pl.CostEstimate(flops=60 * length * lats, bytes_accessed=12 * length * lats * 4, transcendentals=0),
        name="stencil_weights",
    )(fields, thick, zonal_end)


def forward_kernel(
    cap, offset_ref, region_ref, q_ref, edge_ref, weight_ref, source_ref, stays_ref, pick_ref, sign_ref,
    high_ref, low_ref, *rest, first
):
    moved_ref, out_ref, wide, tendency, spectrum = rest[-5:]
    length, lats = q_ref.shape[1:]
    columns = high_ref.shape[1]
    step = 16
    padded = -(-length // step) * step
    for s in range(2):
        wide[s, 6:8] = edge_ref[s, 0:2]
        wide[s, 8:24] = q_ref[s, 0:16]
        wide[s, 40:56] = q_ref[s, length - 16 : length]
        wide[s, 56:58] = edge_ref[s, 2:4]
    stays = stays_ref[...]
    regions = [region_ref[first + 2 * pl.program_id(0) + s] for s in range(2)]
    for start in range(0, length, step):
        rows = min(step, length - start)
        here = slice(start, start + rows)
        for s in range(2):
            q = q_ref[s, here]
            total = source_ref[regions[s], here].astype(jnp.float32) + weight_ref[8, here] * q
            for index, shift in enumerate((-2, -1, 1, 2)):
                if start + shift < 0:
                    moved = wide[s, 8 + shift : 8 + shift + rows]
                elif start + rows + shift > length:
                    moved = wide[s, 56 - rows + shift : 56 + shift]
                else:
                    moved = q_ref[s, start + shift : start + shift + rows]
                total += weight_ref[index, here] * moved
                total += weight_ref[4 + index, here] * pltpu.roll(q, (-shift) % lats, 1)
            moved_ref[s, here] = q + stays * total
            high, low = halves(total)
            tendency[2 * s * padded + start : 2 * s * padded + start + rows] = high
            tendency[(2 * s + 1) * padded + start : (2 * s + 1) * padded + start + rows] = low
    selected = mxu(tendency[...], pick_ref[...])
    turned = []
    for s in range(2):
        at = 2 * s * padded
        x = (selected[at : at + length] + selected[at + padded : at + padded + length]) * sign_ref[...]
        turned.append(x.T)
    x_high, x_low = halves(jnp.concatenate(turned, axis=0))
    with_high = mxu(jnp.concatenate([x_high, x_low], axis=0), high_ref[...])
    spectrum[:, :columns] = with_high[: 2 * FROWS] + with_high[2 * FROWS :] + mxu(x_high, low_ref[...])
    left = lax.broadcasted_iota(jnp.int32, (GROUP, LANES), 1) < 2 * WAVES
    for block in range(columns // (2 * WAVES)):
        lanes = slice(LANES * (block // 2), LANES * (block // 2) + LANES)
        for group in range(FROWS // GROUP):
            a = spectrum[GROUP * group : GROUP * (group + 1), lanes]
            b = spectrum[FROWS + GROUP * group : FROWS + GROUP * (group + 1), lanes]
            if block % 2 == 0:
                tile = jnp.where(left, a, pltpu.roll(b, 2 * WAVES, 1))
            else:
                tile = jnp.where(left, pltpu.roll(a, 2 * WAVES, 1), b)
            out_ref[jnp.minimum(offset_ref[block] + group, cap - 1), 0] = tile


def inverse_kernel(
    cap, offset_ref, end_ref, moved_ref, arrived_ref, held_ref, keep_ref, high_ref, both_ref, flip_ref, put_ref, *rest
):
    out_ref, spectrum = rest[-2:]
    columns = high_ref.shape[1]
    left = lax.broadcasted_iota(jnp.int32, (GROUP, LANES), 1) < 2 * WAVES
    end = lax.broadcasted_iota(jnp.int32, (GROUP, LANES), 0) < GROUP * end_ref[0]
    blocks = columns // (2 * WAVES)

    def load(block, group):
        at = jnp.minimum(offset_ref[block] + group, cap - 1)
        return jnp.where(end, arrived_ref[at, 0], held_ref[at, 0])

    for group in range(FROWS // GROUP):
        for pair in range((blocks + 1) // 2):
            even = load(2 * pair, group)
            odd = load(2 * pair + 1, group) if 2 * pair + 1 < blocks else even
            where = slice(GROUP * group, GROUP * (group + 1)), slice(LANES * pair, LANES * (pair + 1))
            keep = keep_ref[where]
            a = jnp.where(left, even, pltpu.roll(odd, 2 * WAVES, 1))
            b = jnp.where(left, pltpu.roll(even, 2 * WAVES, 1), odd)
            spectrum[(0,) + where] = jnp.where(keep != 0.0, a * keep, 0.0)
            spectrum[(1,) + where] = jnp.where(keep != 0.0, b * keep, 0.0)
    length = high_ref.shape[0]
    s_high, s_low = halves(spectrum[...].reshape(2 * FROWS, -1)[:, :columns])
    last = ((1,), (1,))
    with_high = mxu(both_ref[...], s_high, last)
    back = with_high[:length] + with_high[length:] + mxu(high_ref[...], s_low, last)
    for s in range(2):
        pieces = jnp.concatenate(halves(back[:, s * FROWS : (s + 1) * FROWS] * flip_ref[...]), axis=1)
        out_ref[s] = moved_ref[s] + mxu(pieces, put_ref[...])


RESIDENT = pl.BlockSpec(memory_space=pltpu.VMEM)


def forward(base, size, cap, offsets, regions, tracer, edges, weights, source, stays, pick, sign, high, low, out):
    tags, length, lats = tracer.shape
    pairs = size // 2
    constants = [weights, source, stays, pick, sign, high, low]
    specs = [
        pl.BlockSpec((2, length, lats), lambda p, *_: (base // 2 + p, 0, 0)),
        pl.BlockSpec((2, 4, lats), lambda p, *_: (base // 2 + p, 0, 0)),
    ] + [RESIDENT] * len(constants)
    operands = [offsets, regions, tracer, edges] + constants
    aliases = {}
    if out is not None:
        specs.append(pl.BlockSpec(memory_space=pl.ANY))
        operands.append(out)
        aliases = {len(operands) - 1: 0}
    grid_spec = pltpu.PrefetchScalarGridSpec(
        num_scalar_prefetch=2,
        grid=(pairs,),
        in_specs=specs,
        out_specs=[
            pl.BlockSpec((2, length, lats), lambda p, *_: (base // 2 + p, 0, 0)),
            pl.BlockSpec((cap, 1, GROUP, LANES), lambda p, *_: (0, p, 0, 0)),
        ],
        scratch_shapes=[
            pltpu.VMEM((2, 64, lats), jnp.float32),
            pltpu.VMEM((4 * (-(-length // 16) * 16), lats), jnp.bfloat16),
            pltpu.VMEM((2 * FROWS, -(-high.shape[1] // LANES) * LANES), jnp.float32),
        ],
    )
    flops = size * 2 * length * (2 * lats * FROWS + 3 * high.shape[1] * FROWS)
    return pl.pallas_call(
        functools.partial(forward_kernel, cap, first=base),
        grid_spec=grid_spec,
        out_shape=[
            jax.ShapeDtypeStruct(tracer.shape, jnp.float32),
            jax.ShapeDtypeStruct((cap, pairs, GROUP, LANES), jnp.float32),
        ],
        input_output_aliases=aliases,
        compiler_params=pltpu.CompilerParams(vmem_limit_bytes=VMEM),
        cost_estimate=pl.CostEstimate(flops=flops, bytes_accessed=5 * size * length * lats * 4, transcendentals=0),
        name="step_and_transform",
    )(*operands)


def inverse(base, size, cap, offsets, end, out, arrived, held, keep, high, both, flip, put):
    tags, length, lats = out.shape
    pairs = size // 2
    constants = [keep, high, both, flip, put]
    specs = [
        pl.BlockSpec((2, length, lats), lambda p, *_: (base // 2 + p, 0, 0)),
        pl.BlockSpec((cap, 1, GROUP, LANES), lambda p, *_: (0, p, 0, 0)),
        pl.BlockSpec((cap, 1, GROUP, LANES), lambda p, *_: (0, p, 0, 0)),
    ] + [RESIDENT] * len(constants)
    operands = [offsets, end, out, arrived, held] + constants
    grid_spec = pltpu.PrefetchScalarGridSpec(
        num_scalar_prefetch=2,
        grid=(pairs,),
        in_specs=specs,
        out_specs=pl.BlockSpec((2, length, lats), lambda p, *_: (base // 2 + p, 0, 0)),
        scratch_shapes=[pltpu.VMEM((2, FROWS, keep.shape[1]), jnp.float32)],
    )
    flops = size * 2 * length * (2 * lats * FROWS + 3 * high.shape[1] * FROWS)
    return pl.pallas_call(
        functools.partial(inverse_kernel, cap),
        grid_spec=grid_spec,
        out_shape=jax.ShapeDtypeStruct(out.shape, jnp.float32),
        input_output_aliases={2: 0},
        compiler_params=pltpu.CompilerParams(vmem_limit_bytes=VMEM),
        cost_estimate=pl.CostEstimate(flops=flops, bytes_accessed=2 * size * length * lats * 4, transcendentals=0),
        name="restore",
    )(*operands)


def sum_over_lon(packed, count, place):
    middle = count // 2
    total = packed
    for hop in range(middle - 1):
        inward = [(hop, hop + 1), (count - 1 - hop, count - 2 - hop)]
        total = total + lax.ppermute(total, "lon", inward)
    total = total + lax.ppermute(total, "lon", [(middle - 1, middle), (middle, middle - 1)])
    for hop in range(middle - 2, -1, -1):
        outward = [(hop + 1, hop), (count - 2 - hop, count - 1 - hop)]
        arrived = lax.ppermute(total, "lon", outward)
        total = jnp.where((place == hop) | (place == count - 1 - hop), arrived, total)
    return total


def plain_pipeline(chunks, forward_at, inverse_at, place, count, offsets):
    out = None
    for chunk in range(chunks):
        out, packed = forward_at(chunk, out, offsets)
        total = sum_over_lon(packed, count, place)
        out = inverse_at(chunk, out, total, total, offsets)
    return out


def stepped_pipeline(chunks, forward_at, inverse_at, place, count, offsets):
    swap = [(0, 1), (1, 0), (2, 3), (3, 2)]
    cross = [(1, 2), (2, 1)]
    end = (place == 0) | (place == count - 1)
    own, back = {}, {}
    out, own[0] = forward_at(0, None, offsets)
    pair_sum = swapped = crossed = sent = None
    done = 0
    for t in range(chunks + 3):
        if t >= 3:
            back[t - 3] = swapped, sent
        total = None if crossed is None else pair_sum + crossed
        here = own.get(t)
        if here is None:
            sent = total
        else:
            sent = here if total is None else jnp.where(end, here, total)
        pair_sum = own[t - 1] + swapped if 1 <= t <= chunks else None
        token = offsets
        if t < chunks + 2:
            sending = [x for x in (sent, pair_sum) if x is not None]
            token, out, *sending = lax.optimization_barrier((offsets, out, *sending))
            if pair_sum is not None:
                pair_sum = sending.pop()
            if sent is not None:
                sent = sending.pop()
            swapped = None if sent is None else lax.ppermute(sent, "lon", swap)
            crossed = None if pair_sum is None else lax.ppermute(pair_sum, "lon", cross)
        if t + 1 < chunks:
            out, own[t + 1] = forward_at(t + 1, out, token)
        quota = chunks if t == chunks + 2 else -(-(chunks - 1 - done) // (chunks + 2 - t)) if t >= chunks - 1 else 0
        while quota and done in back:
            out = inverse_at(done, out, *back[done], token)
            done += 1
            quota -= 1
    return out


def ring_edges(first, last, count):
    forward_ring = [(i, (i + 1) % count) for i in range(count)]
    backward_ring = [((i + 1) % count, i) for i in range(count)]
    before = lax.ppermute(last, "lon", forward_ring)
    after = lax.ppermute(first, "lon", backward_ring)
    return before, after


def body(tracer, courant, thickness, emission, region_map, filter_mask, cutoff):
    tracer = tracer[:, 0]
    courant, thickness = courant[:, 0], thickness[0]
    tags, length, lats = tracer.shape
    count = lax.axis_size("lon")
    place = lax.axis_index("lon")
    full = length * count
    nyquist = full // 2
    groups = FROWS // GROUP
    backward_ring = [((i + 1) % count, i) for i in range(count)]

    flipped = cutoff > nyquist - 1 - cutoff
    reach = jnp.minimum(cutoff, nyquist - 1 - cutoff)
    masked = filter_mask == 1
    score = jnp.where(masked, reach + 2, 0)
    lat = jnp.arange(lats, dtype=jnp.int32)
    ahead = (score[None, :] > score[:, None]) | ((score[None, :] == score[:, None]) & (lat[None, :] < lat[:, None]))
    rank = jnp.sum(ahead.astype(jnp.int32), axis=1)
    chosen = rank[:, None] == jnp.arange(FROWS, dtype=jnp.int32)[None, :]
    row_reach = jnp.sum(jnp.where(chosen, reach[:, None], 0), axis=0)
    row_flipped = jnp.any(chosen & flipped[:, None], axis=0)
    one_hot = chosen.astype(jnp.bfloat16)
    put = one_hot.T

    blocks = nyquist // 2 // WAVES
    starts = jnp.arange(blocks, dtype=jnp.int32) * WAVES
    needed = jnp.sum((row_reach[None, :] >= starts[:, None]).astype(jnp.int32), axis=1)
    taken = (needed + GROUP - 1) // GROUP
    offsets = jnp.sum(
        jnp.where(jnp.arange(blocks)[None, :] < jnp.arange(blocks)[:, None], taken[None, :], 0), axis=1
    ).astype(jnp.int32)
    used = jnp.sum(taken)

    lane = jnp.arange(-(-blocks * 2 * WAVES // LANES) * LANES, dtype=jnp.int32)
    wave = lane // (2 * WAVES) * WAVES + lane % WAVES
    scaling = jnp.where(wave == 0, 1.0 / full, 2.0 / full).astype(jnp.float32)
    keep = jnp.where(wave[None, :] <= row_reach[:, None], scaling[None, :], 0.0)
    high, low = (
        lax.dynamic_slice_in_dim(jnp.asarray(table), place * length, length, 0) for table in wave_table(full)
    )
    odd = (place * length + jnp.arange(length, dtype=jnp.int32)) % 2 == 1
    sign = jnp.where(odd[:, None] & row_flipped[None, :], -1.0, 1.0).astype(jnp.float32)
    flip = jnp.where(row_flipped[None, :], -sign, sign)
    stays = jnp.where(masked & ~flipped, 0.0, 1.0).astype(jnp.float32)[None, :]

    largest = blocks * groups
    both = jnp.concatenate([high, low])
    put = jnp.concatenate([put, put])
    is_end = ((place == 0) | (place == count - 1)).astype(jnp.int32).reshape(1)
    sizes = [CHUNK] * (tags // CHUNK)
    bases = [sum(sizes[:i]) for i in range(len(sizes))]

    tag_count, tag = lax.axis_size("tag"), lax.axis_index("tag")
    if tag_count == 2:
        cross = [(0, 1), (1, 0)]
        other, other_thick = lax.ppermute(courant, "tag", cross), lax.ppermute(thickness, "tag", cross)
        ahead_zonal = courant[0, :1]
        same = lax.ppermute(ahead_zonal, "lon", backward_ring)
        skew = lax.ppermute(ahead_zonal, ("lon", "tag"), [((i + 1) % count * 2, i * 2 + 1) for i in range(count)])
        zonal_end = jnp.where(tag == 0, same, skew)

        def in_order(mine, theirs, axis):
            return jnp.concatenate([jnp.where(tag == 0, mine, theirs), jnp.where(tag == 0, theirs, mine)], axis=axis)

        gathered, thick = in_order(courant, other, 1), in_order(thickness, other_thick, 0)
    else:
        gathered = lax.all_gather(courant, "tag", axis=1, tiled=True)
        thick = lax.all_gather(thickness, "tag", axis=0, tiled=True)
        zonal_end = lax.all_gather(lax.ppermute(courant[0, :1], "lon", backward_ring), "tag")[0]
    edges = jnp.concatenate(ring_edges(tracer[:, :2], tracer[:, length - 2 :], count), axis=1)

    def run(cap):
        weights, keep_, both_, flip_, put_, edges_ = lax.optimization_barrier((stencil_weights(gathered, thick, zonal_end), keep, both, flip, put, edges))

        def forward_at(chunk, out, offsets):
            return forward(
                bases[chunk], sizes[chunk], cap, offsets, region_map, tracer, edges_, weights, emission, stays, one_hot,
                sign, high, low, out,
            )

        def inverse_at(chunk, out, arrived, held, offsets):
            return inverse(
                bases[chunk], sizes[chunk], cap, offsets, is_end, out, arrived, held, keep_, high, both_, flip_, put_
            )

        pipeline = stepped_pipeline if count == 4 else plain_pipeline
        return pipeline(len(sizes), forward_at, inverse_at, place, count, offsets)

    caps = [int(share * largest) + 1 for share in CAPS]
    if len(caps) == 1:
        out = run(caps[0])
    else:
        index = sum((used >= cap).astype(jnp.int32) for cap in caps[:-1])
        out = lax.switch(index, [functools.partial(run, cap) for cap in caps])
    return out[:, None]


def solution(mesh):
    in_specs = (
        P(("runs", "tag"), "lev", "lon", None),
        P(None, ("runs", "lev"), ("lon", "tag"), None),
        P(("runs", "lev"), ("lon", "tag"), None),
        P(None, "lon", None),
        P(("runs", "tag")),
        P(),
        P(),
    )
    out_specs = P(("runs", "tag"), "lev", "lon", None)
    return jax.shard_map(body, mesh=mesh, in_specs=in_specs, out_specs=out_specs, check_vma=False)
```

```python
import functools

import jax
import jax.numpy as jnp
import ml_dtypes
import numpy as np
from jax import lax
from jax.experimental import pallas as pl
from jax.experimental.pallas import tpu as pltpu
from jax.sharding import PartitionSpec as P

FROWS = 128
GROUP = 8
WAVES = 32
LANES = 128
CHUNK = 4
CAPS = (0.605, 0.66, 1.0)
VMEM = 18 * 1024 * 1024


def wave_table(length):
    waves = np.arange(length // 4).reshape(-1, WAVES)
    phase = (np.arange(length)[:, None, None] * waves[None]) % length
    angle = phase * (2.0 * np.pi / length)
    table = np.concatenate([np.cos(angle), np.sin(angle)], axis=-1).reshape(length, -1)
    high = table.astype(ml_dtypes.bfloat16)
    low = (table - high.astype(np.float64)).astype(ml_dtypes.bfloat16)
    return high, low


def halves(value):
    high = value.astype(jnp.bfloat16)
    low = (value - high.astype(jnp.float32)).astype(jnp.bfloat16)
    return high, low


def mxu(left, right, contract=((1,), (0,))):
    return lax.dot_general(left, right, (contract, ((), ())), preferred_element_type=jnp.float32)


def divergence(face, next_face):
    half, next_half = 0.5 * jnp.abs(face), 0.5 * jnp.abs(next_face)
    return (
        face / 12.0,
        -next_face / 12.0 - 7.0 / 12.0 * face - half,
        7.0 / 12.0 * (next_face - face) + half + next_half,
        7.0 / 12.0 * next_face - next_half + face / 12.0,
        -next_face / 12.0,
    )


def weight_kernel(fields_ref, thick_ref, end_ref, out_ref, wide):
    length, lats = thick_ref.shape
    wide[0:length] = fields_ref[0]
    wide[length : length + 1] = end_ref[...]
    lat = lax.broadcasted_iota(jnp.int32, (8, lats), 1)
    for start in range(0, length, 8):
        here = slice(start, start + 8)
        merid = jnp.where(lat > 0, fields_ref[1, here], 0.0)
        north = jnp.where(lat < lats - 1, pltpu.roll(merid, lats - 1, 1), 0.0)
        factor = -1.0 / thick_ref[here]
        along = divergence(wide[here], wide[start + 1 : start + 9])
        across = divergence(merid, north)
        for index, part in enumerate((along[0], along[1], along[3], along[4])):
            out_ref[index, here] = part * factor
        inside = (lat >= 2, lat >= 1, lat <= lats - 2, lat <= lats - 3)
        for index, part in enumerate((across[0], across[1], across[3], across[4])):
            out_ref[4 + index, here] = jnp.where(inside[index], part * factor, 0.0)
        out_ref[8, here] = (along[2] + across[2]) * factor


def stencil_weights(fields, thick, zonal_end):
    length, lats = thick.shape
    return pl.pallas_call(
        weight_kernel,
        in_specs=[RESIDENT] * 3,
        out_specs=RESIDENT,
        out_shape=jax.ShapeDtypeStruct((9, length, lats), jnp.float32),
        scratch_shapes=[pltpu.VMEM((length + 8, lats), jnp.float32)],
        compiler_params=pltpu.CompilerParams(vmem_limit_bytes=VMEM),
        cost_estimate=pl.CostEstimate(flops=60 * length * lats, bytes_accessed=12 * length * lats * 4, transcendentals=0),
        name="stencil_weights",
    )(fields, thick, zonal_end)


def forward_kernel(
    cap, offset_ref, region_ref, q_ref, edge_ref, weight_ref, source_ref, stays_ref, pick_ref, sign_ref,
    high_ref, low_ref, *rest, first
):
    moved_ref, out_ref, wide, tendency, spectrum = rest[-5:]
    length, lats = q_ref.shape[1:]
    columns = high_ref.shape[1]
    step = 16
    padded = -(-length // step) * step
    for s in range(2):
        wide[s, 6:8] = edge_ref[s, 0:2]
        wide[s, 8:24] = q_ref[s, 0:16]
        wide[s, 40:56] = q_ref[s, length - 16 : length]
        wide[s, 56:58] = edge_ref[s, 2:4]
    stays = stays_ref[...]
    regions = [region_ref[first + 2 * pl.program_id(0) + s] for s in range(2)]
    for start in range(0, length, step):
        rows = min(step, length - start)
        here = slice(start, start + rows)
        for s in range(2):
            q = q_ref[s, here]
            total = source_ref[regions[s], here].astype(jnp.float32) + weight_ref[8, here] * q
            for index, shift in enumerate((-2, -1, 1, 2)):
                if start + shift < 0:
                    moved = wide[s, 8 + shift : 8 + shift + rows]
                elif start + rows + shift > length:
                    moved = wide[s, 56 - rows + shift : 56 + shift]
                else:
                    moved = q_ref[s, start + shift : start + shift + rows]
                total += weight_ref[index, here] * moved
                total += weight_ref[4 + index, here] * pltpu.roll(q, (-shift) % lats, 1)
            moved_ref[s, here] = q + stays * total
            high, low = halves(total)
            tendency[2 * s * padded + start : 2 * s * padded + start + rows] = high
            tendency[(2 * s + 1) * padded + start : (2 * s + 1) * padded + start + rows] = low
    selected = mxu(tendency[...], pick_ref[...])
    turned = []
    for s in range(2):
        at = 2 * s * padded
        x = (selected[at : at + length] + selected[at + padded : at + padded + length]) * sign_ref[...]
        turned.append(x.T)
    x_high, x_low = halves(jnp.concatenate(turned, axis=0))
    with_high = mxu(jnp.concatenate([x_high, x_low], axis=0), high_ref[...])
    spectrum[:, :columns] = with_high[: 2 * FROWS] + with_high[2 * FROWS :] + mxu(x_high, low_ref[...])
    left = lax.broadcasted_iota(jnp.int32, (GROUP, LANES), 1) < 2 * WAVES
    for block in range(columns // (2 * WAVES)):
        lanes = slice(LANES * (block // 2), LANES * (block // 2) + LANES)
        for group in range(FROWS // GROUP):
            a = spectrum[GROUP * group : GROUP * (group + 1), lanes]
            b = spectrum[FROWS + GROUP * group : FROWS + GROUP * (group + 1), lanes]
            if block % 2 == 0:
                tile = jnp.where(left, a, pltpu.roll(b, 2 * WAVES, 1))
            else:
                tile = jnp.where(left, pltpu.roll(a, 2 * WAVES, 1), b)
            out_ref[jnp.minimum(offset_ref[block] + group, cap - 1), 0] = tile


def inverse_kernel(cap, pairs, many, offset_ref, end_ref, moved_ref, *rest):
    packed_refs = rest[: 2 * many]
    keep_ref, high_ref, both_ref, flip_ref, put_ref, out_ref, spectrum = rest[2 * many :]
    columns = high_ref.shape[1]
    left = lax.broadcasted_iota(jnp.int32, (GROUP, LANES), 1) < 2 * WAVES
    end = lax.broadcasted_iota(jnp.int32, (GROUP, LANES), 0) < GROUP * end_ref[0]
    blocks = columns // (2 * WAVES)

    def unpack(arrived_ref, held_ref):
        def load(block, group):
            at = jnp.minimum(offset_ref[block] + group, cap - 1)
            return jnp.where(end, arrived_ref[at, 0], held_ref[at, 0])

        for group in range(FROWS // GROUP):
            for pair in range((blocks + 1) // 2):
                even = load(2 * pair, group)
                odd = load(2 * pair + 1, group) if 2 * pair + 1 < blocks else even
                where = slice(GROUP * group, GROUP * (group + 1)), slice(LANES * pair, LANES * (pair + 1))
                keep = keep_ref[where]
                a = jnp.where(left, even, pltpu.roll(odd, 2 * WAVES, 1))
                b = jnp.where(left, pltpu.roll(even, 2 * WAVES, 1), odd)
                spectrum[(0,) + where] = jnp.where(keep != 0.0, a * keep, 0.0)
                spectrum[(1,) + where] = jnp.where(keep != 0.0, b * keep, 0.0)

    if many == 1:
        unpack(*packed_refs)
    else:
        for index in range(many):
            pl.when(pl.program_id(0) // pairs == index)(
                functools.partial(unpack, packed_refs[2 * index], packed_refs[2 * index + 1])
            )
    length = high_ref.shape[0]
    s_high, s_low = halves(spectrum[...].reshape(2 * FROWS, -1)[:, :columns])
    last = ((1,), (1,))
    with_high = mxu(both_ref[...], s_high, last)
    back = with_high[:length] + with_high[length:] + mxu(high_ref[...], s_low, last)
    for s in range(2):
        pieces = jnp.concatenate(halves(back[:, s * FROWS : (s + 1) * FROWS] * flip_ref[...]), axis=1)
        out_ref[s] = moved_ref[s] + mxu(pieces, put_ref[...])


RESIDENT = pl.BlockSpec(memory_space=pltpu.VMEM)


def forward(base, size, cap, offsets, regions, tracer, edges, weights, source, stays, pick, sign, high, low, out):
    tags, length, lats = tracer.shape
    pairs = size // 2
    constants = [weights, source, stays, pick, sign, high, low]
    specs = [
        pl.BlockSpec((2, length, lats), lambda p, *_: (base // 2 + p, 0, 0)),
        pl.BlockSpec((2, 4, lats), lambda p, *_: (base // 2 + p, 0, 0)),
    ] + [RESIDENT] * len(constants)
    operands = [offsets, regions, tracer, edges] + constants
    aliases = {}
    if out is not None:
        specs.append(pl.BlockSpec(memory_space=pl.ANY))
        operands.append(out)
        aliases = {len(operands) - 1: 0}
    grid_spec = pltpu.PrefetchScalarGridSpec(
        num_scalar_prefetch=2,
        grid=(pairs,),
        in_specs=specs,
        out_specs=[
            pl.BlockSpec((2, length, lats), lambda p, *_: (base // 2 + p, 0, 0)),
            pl.BlockSpec((cap, 1, GROUP, LANES), lambda p, *_: (0, p, 0, 0)),
        ],
        scratch_shapes=[
            pltpu.VMEM((2, 64, lats), jnp.float32),
            pltpu.VMEM((4 * (-(-length // 16) * 16), lats), jnp.bfloat16),
            pltpu.VMEM((2 * FROWS, -(-high.shape[1] // LANES) * LANES), jnp.float32),
        ],
    )
    flops = size * 2 * length * (2 * lats * FROWS + 3 * high.shape[1] * FROWS)
    return pl.pallas_call(
        functools.partial(forward_kernel, cap, first=base),
        grid_spec=grid_spec,
        out_shape=[
            jax.ShapeDtypeStruct(tracer.shape, jnp.float32),
            jax.ShapeDtypeStruct((cap, pairs, GROUP, LANES), jnp.float32),
        ],
        input_output_aliases=aliases,
        compiler_params=pltpu.CompilerParams(vmem_limit_bytes=VMEM),
        cost_estimate=pl.CostEstimate(flops=flops, bytes_accessed=5 * size * length * lats * 4, transcendentals=0),
        name="step_and_transform",
    )(*operands)


def inverse(base, size, cap, offsets, end, out, packed, keep, high, both, flip, put):
    tags, length, lats = out.shape
    pairs, many = size // 2, len(packed)
    constants = [keep, high, both, flip, put]
    specs = [pl.BlockSpec((2, length, lats), lambda p, *_: (base // 2 + p, 0, 0))]
    for index in range(many):
        at = lambda p, *_, start=index * pairs: (0, jnp.clip(p - start, 0, pairs - 1), 0, 0)
        specs += [pl.BlockSpec((cap, 1, GROUP, LANES), at)] * 2
    grid_spec = pltpu.PrefetchScalarGridSpec(
        num_scalar_prefetch=2,
        grid=(many * pairs,),
        in_specs=specs + [RESIDENT] * len(constants),
        out_specs=pl.BlockSpec((2, length, lats), lambda p, *_: (base // 2 + p, 0, 0)),
        scratch_shapes=[pltpu.VMEM((2, FROWS, keep.shape[1]), jnp.float32)],
    )
    flops = many * size * 2 * length * (2 * lats * FROWS + 3 * high.shape[1] * FROWS)
    return pl.pallas_call(
        functools.partial(inverse_kernel, cap, pairs, many),
        grid_spec=grid_spec,
        out_shape=jax.ShapeDtypeStruct(out.shape, jnp.float32),
        input_output_aliases={2: 0},
        compiler_params=pltpu.CompilerParams(vmem_limit_bytes=VMEM),
        cost_estimate=pl.CostEstimate(
            flops=flops, bytes_accessed=2 * many * size * length * lats * 4, transcendentals=0
        ),
        name="restore",
    )(offsets, end, out, *[array for pair in packed for array in pair], *constants)


def sum_over_lon(packed, count, place):
    middle = count // 2
    total = packed
    for hop in range(middle - 1):
        inward = [(hop, hop + 1), (count - 1 - hop, count - 2 - hop)]
        total = total + lax.ppermute(total, "lon", inward)
    total = total + lax.ppermute(total, "lon", [(middle - 1, middle), (middle, middle - 1)])
    for hop in range(middle - 2, -1, -1):
        outward = [(hop + 1, hop), (count - 2 - hop, count - 1 - hop)]
        arrived = lax.ppermute(total, "lon", outward)
        total = jnp.where((place == hop) | (place == count - 1 - hop), arrived, total)
    return total


def plain_pipeline(chunks, forward_at, inverse_at, place, count, offsets):
    out = None
    for chunk in range(chunks):
        out, packed = forward_at(chunk, out, offsets)
        total = sum_over_lon(packed, count, place)
        out = inverse_at(chunk, out, [(total, total)], offsets)
    return out


def stepped_pipeline(chunks, forward_at, inverse_at, place, count, offsets):
    swap = [(0, 1), (1, 0), (2, 3), (3, 2)]
    cross = [(1, 2), (2, 1)]
    end = (place == 0) | (place == count - 1)
    own, back = {}, {}
    out, own[0] = forward_at(0, None, offsets)
    pair_sum = swapped = crossed = sent = None
    done = 0
    for t in range(chunks + 3):
        if t >= 3:
            back[t - 3] = swapped, sent
        total = None if crossed is None else pair_sum + crossed
        here = own.get(t)
        if here is None:
            sent = total
        else:
            sent = here if total is None else jnp.where(end, here, total)
        pair_sum = own[t - 1] + swapped if 1 <= t <= chunks else None
        token = offsets
        if t < chunks + 2:
            sending = [x for x in (sent, pair_sum) if x is not None]
            token, out, *sending = lax.optimization_barrier((offsets, out, *sending))
            if pair_sum is not None:
                pair_sum = sending.pop()
            if sent is not None:
                sent = sending.pop()
            swapped = None if sent is None else lax.ppermute(sent, "lon", swap)
            crossed = None if pair_sum is None else lax.ppermute(pair_sum, "lon", cross)
        if t + 1 < chunks:
            out, own[t + 1] = forward_at(t + 1, out, token)
        quota = chunks if t == chunks + 2 else -(-(chunks - 1 - done) // (chunks + 2 - t)) if t >= chunks - 1 else 0
        ready = [back[i] for i in range(done, min(done + quota, chunks)) if i in back]
        if ready:
            out = inverse_at(done, out, ready, token)
            done += len(ready)
    return out


def ring_edges(first, last, count):
    forward_ring = [(i, (i + 1) % count) for i in range(count)]
    backward_ring = [((i + 1) % count, i) for i in range(count)]
    before = lax.ppermute(last, "lon", forward_ring)
    after = lax.ppermute(first, "lon", backward_ring)
    return before, after


def body(tracer, courant, thickness, emission, region_map, filter_mask, cutoff):
    tracer = tracer[:, 0]
    courant, thickness = courant[:, 0], thickness[0]
    tags, length, lats = tracer.shape
    count = lax.axis_size("lon")
    place = lax.axis_index("lon")
    full = length * count
    nyquist = full // 2
    groups = FROWS // GROUP
    backward_ring = [((i + 1) % count, i) for i in range(count)]

    flipped = cutoff > nyquist - 1 - cutoff
    reach = jnp.minimum(cutoff, nyquist - 1 - cutoff)
    masked = filter_mask == 1
    score = jnp.where(masked, reach + 2, 0)
    lat = jnp.arange(lats, dtype=jnp.int32)
    ahead = (score[None, :] > score[:, None]) | ((score[None, :] == score[:, None]) & (lat[None, :] < lat[:, None]))
    rank = jnp.sum(ahead.astype(jnp.int32), axis=1)
    chosen = rank[:, None] == jnp.arange(FROWS, dtype=jnp.int32)[None, :]
    row_reach = jnp.sum(jnp.where(chosen, reach[:, None], 0), axis=0)
    row_flipped = jnp.any(chosen & flipped[:, None], axis=0)
    one_hot = chosen.astype(jnp.bfloat16)
    put = one_hot.T

    blocks = nyquist // 2 // WAVES
    starts = jnp.arange(blocks, dtype=jnp.int32) * WAVES
    needed = jnp.sum((row_reach[None, :] >= starts[:, None]).astype(jnp.int32), axis=1)
    taken = (needed + GROUP - 1) // GROUP
    offsets = jnp.sum(
        jnp.where(jnp.arange(blocks)[None, :] < jnp.arange(blocks)[:, None], taken[None, :], 0), axis=1
    ).astype(jnp.int32)
    used = jnp.sum(taken)

    lane = jnp.arange(-(-blocks * 2 * WAVES // LANES) * LANES, dtype=jnp.int32)
    wave = lane // (2 * WAVES) * WAVES + lane % WAVES
    scaling = jnp.where(wave == 0, 1.0 / full, 2.0 / full).astype(jnp.float32)
    keep = jnp.where(wave[None, :] <= row_reach[:, None], scaling[None, :], 0.0)
    high, low = (
        lax.dynamic_slice_in_dim(jnp.asarray(table), place * length, length, 0) for table in wave_table(full)
    )
    odd = (place * length + jnp.arange(length, dtype=jnp.int32)) % 2 == 1
    sign = jnp.where(odd[:, None] & row_flipped[None, :], -1.0, 1.0).astype(jnp.float32)
    flip = jnp.where(row_flipped[None, :], -sign, sign)
    stays = jnp.where(masked & ~flipped, 0.0, 1.0).astype(jnp.float32)[None, :]

    largest = blocks * groups
    both = jnp.concatenate([high, low])
    put = jnp.concatenate([put, put])
    is_end = ((place == 0) | (place == count - 1)).astype(jnp.int32).reshape(1)
    sizes = [CHUNK] * (tags // CHUNK)
    bases = [sum(sizes[:i]) for i in range(len(sizes))]

    tag_count, tag = lax.axis_size("tag"), lax.axis_index("tag")
    if tag_count == 2:
        cross = [(0, 1), (1, 0)]
        other, other_thick = lax.ppermute(courant, "tag", cross), lax.ppermute(thickness, "tag", cross)
        ahead_zonal = courant[0, :1]
        same = lax.ppermute(ahead_zonal, "lon", backward_ring)
        skew = lax.ppermute(ahead_zonal, ("lon", "tag"), [((i + 1) % count * 2, i * 2 + 1) for i in range(count)])
        zonal_end = jnp.where(tag == 0, same, skew)

        def in_order(mine, theirs, axis):
            return jnp.concatenate([jnp.where(tag == 0, mine, theirs), jnp.where(tag == 0, theirs, mine)], axis=axis)

        gathered, thick = in_order(courant, other, 1), in_order(thickness, other_thick, 0)
    else:
        gathered = lax.all_gather(courant, "tag", axis=1, tiled=True)
        thick = lax.all_gather(thickness, "tag", axis=0, tiled=True)
        zonal_end = lax.all_gather(lax.ppermute(courant[0, :1], "lon", backward_ring), "tag")[0]
    edges = jnp.concatenate(ring_edges(tracer[:, :2], tracer[:, length - 2 :], count), axis=1)

    def run(cap):
        weights, keep_, both_, flip_, put_, edges_ = lax.optimization_barrier((stencil_weights(gathered, thick, zonal_end), keep, both, flip, put, edges))

        def forward_at(chunk, out, offsets):
            return forward(
                bases[chunk], sizes[chunk], cap, offsets, region_map, tracer, edges_, weights, emission, stays, one_hot,
                sign, high, low, out,
            )

        def inverse_at(chunk, out, packed, offsets):
            return inverse(bases[chunk], CHUNK, cap, offsets, is_end, out, packed, keep_, high, both_, flip_, put_)

        pipeline = stepped_pipeline if count == 4 else plain_pipeline
        return pipeline(len(sizes), forward_at, inverse_at, place, count, offsets)

    caps = [int(share * largest) + 1 for share in CAPS]
    if len(caps) == 1:
        out = run(caps[0])
    else:
        index = sum((used >= cap).astype(jnp.int32) for cap in caps[:-1])
        out = lax.switch(index, [functools.partial(run, cap) for cap in caps])
    return out[:, None]


def solution(mesh):
    in_specs = (
        P(("runs", "tag"), "lev", "lon", None),
        P(None, ("runs", "lev"), ("lon", "tag"), None),
        P(("runs", "lev"), ("lon", "tag"), None),
        P(None, "lon", None),
        P(("runs", "tag")),
        P(),
        P(),
    )
    out_specs = P(("runs", "tag"), "lev", "lon", None)
    return jax.shard_map(body, mesh=mesh, in_specs=in_specs, out_specs=out_specs, check_vma=False)
```

```python
import functools

import jax
import jax.numpy as jnp
import ml_dtypes
import numpy as np
from jax import lax
from jax.experimental import pallas as pl
from jax.experimental.pallas import tpu as pltpu
from jax.sharding import PartitionSpec as P

FROWS = 128
GROUP = 8
WAVES = 32
LANES = 128
CHUNK = 4
CAPS = (0.605, 0.66, 1.0)
VMEM = 32 * 1024 * 1024


def wave_table(length):
    waves = np.arange(length // 4).reshape(-1, WAVES)
    phase = (np.arange(length)[:, None, None] * waves[None]) % length
    angle = phase * (2.0 * np.pi / length)
    table = np.concatenate([np.cos(angle), np.sin(angle)], axis=-1).reshape(length, -1)
    high = table.astype(ml_dtypes.bfloat16)
    low = (table - high.astype(np.float64)).astype(ml_dtypes.bfloat16)
    return high, low


def halves(value):
    high = value.astype(jnp.bfloat16)
    low = (value - high.astype(jnp.float32)).astype(jnp.bfloat16)
    return high, low


def mxu(left, right, contract=((1,), (0,))):
    return lax.dot_general(left, right, (contract, ((), ())), preferred_element_type=jnp.float32)


def divergence(face, next_face):
    half, next_half = 0.5 * jnp.abs(face), 0.5 * jnp.abs(next_face)
    return (
        face / 12.0,
        -next_face / 12.0 - 7.0 / 12.0 * face - half,
        7.0 / 12.0 * (next_face - face) + half + next_half,
        7.0 / 12.0 * next_face - next_half + face / 12.0,
        -next_face / 12.0,
    )


def weight_kernel(fields_ref, thick_ref, end_ref, out_ref, wide):
    length, lats = thick_ref.shape
    wide[0:length] = fields_ref[0]
    wide[length : length + 1] = end_ref[...]
    lat = lax.broadcasted_iota(jnp.int32, (8, lats), 1)
    for start in range(0, length, 8):
        here = slice(start, start + 8)
        merid = jnp.where(lat > 0, fields_ref[1, here], 0.0)
        north = jnp.where(lat < lats - 1, pltpu.roll(merid, lats - 1, 1), 0.0)
        factor = -1.0 / thick_ref[here]
        along = divergence(wide[here], wide[start + 1 : start + 9])
        across = divergence(merid, north)
        for index, part in enumerate((along[0], along[1], along[3], along[4])):
            out_ref[index, here] = part * factor
        inside = (lat >= 2, lat >= 1, lat <= lats - 2, lat <= lats - 3)
        for index, part in enumerate((across[0], across[1], across[3], across[4])):
            out_ref[4 + index, here] = jnp.where(inside[index], part * factor, 0.0)
        out_ref[8, here] = (along[2] + across[2]) * factor


def stencil_weights(fields, thick, zonal_end):
    length, lats = thick.shape
    return pl.pallas_call(
        weight_kernel,
        in_specs=[RESIDENT] * 3,
        out_specs=RESIDENT,
        out_shape=jax.ShapeDtypeStruct((9, length, lats), jnp.float32),
        scratch_shapes=[pltpu.VMEM((length + 8, lats), jnp.float32)],
        compiler_params=pltpu.CompilerParams(vmem_limit_bytes=VMEM),
        cost_estimate=pl.CostEstimate(flops=60 * length * lats, bytes_accessed=12 * length * lats * 4, transcendentals=0),
        name="stencil_weights",
    )(fields, thick, zonal_end)


def forward_kernel(
    cap, offset_ref, region_ref, q_ref, edge_ref, weight_ref, source_ref, stays_ref, pick_ref, sign_ref,
    high_ref, low_ref, *rest, first
):
    moved_ref, out_ref, wide, tendency, spectrum = rest[-5:]
    length, lats = q_ref.shape[1:]
    columns = high_ref.shape[1]
    step = 16
    padded = -(-length // step) * step
    for s in range(2):
        wide[s, 6:8] = edge_ref[s, 0:2]
        wide[s, 8:24] = q_ref[s, 0:16]
        wide[s, 40:56] = q_ref[s, length - 16 : length]
        wide[s, 56:58] = edge_ref[s, 2:4]
    stays = stays_ref[...]
    regions = [region_ref[first + 2 * pl.program_id(0) + s] for s in range(2)]
    for start in range(0, length, step):
        rows = min(step, length - start)
        here = slice(start, start + rows)
        for s in range(2):
            q = q_ref[s, here]
            total = source_ref[regions[s], here].astype(jnp.float32) + weight_ref[8, here] * q
            for index, shift in enumerate((-2, -1, 1, 2)):
                if start + shift < 0:
                    moved = wide[s, 8 + shift : 8 + shift + rows]
                elif start + rows + shift > length:
                    moved = wide[s, 56 - rows + shift : 56 + shift]
                else:
                    moved = q_ref[s, start + shift : start + shift + rows]
                total += weight_ref[index, here] * moved
                total += weight_ref[4 + index, here] * pltpu.roll(q, (-shift) % lats, 1)
            moved_ref[s, here] = q + stays * total
            high, low = halves(total)
            tendency[2 * s * padded + start : 2 * s * padded + start + rows] = high
            tendency[(2 * s + 1) * padded + start : (2 * s + 1) * padded + start + rows] = low
    selected = mxu(tendency[...], pick_ref[...])
    turned = []
    for s in range(2):
        at = 2 * s * padded
        x = (selected[at : at + length] + selected[at + padded : at + padded + length]) * sign_ref[...]
        turned.append(x.T)
    x_high, x_low = halves(jnp.concatenate(turned, axis=0))
    with_high = mxu(jnp.concatenate([x_high, x_low], axis=0), high_ref[...])
    spectrum[:, :columns] = with_high[: 2 * FROWS] + with_high[2 * FROWS :] + mxu(x_high, low_ref[...])
    left = lax.broadcasted_iota(jnp.int32, (GROUP, LANES), 1) < 2 * WAVES
    for block in range(columns // (2 * WAVES)):
        lanes = slice(LANES * (block // 2), LANES * (block // 2) + LANES)
        for group in range(FROWS // GROUP):
            a = spectrum[GROUP * group : GROUP * (group + 1), lanes]
            b = spectrum[FROWS + GROUP * group : FROWS + GROUP * (group + 1), lanes]
            if block % 2 == 0:
                tile = jnp.where(left, a, pltpu.roll(b, 2 * WAVES, 1))
            else:
                tile = jnp.where(left, pltpu.roll(a, 2 * WAVES, 1), b)
            out_ref[jnp.minimum(offset_ref[block] + group, cap - 1), 0] = tile


def inverse_kernel(cap, pairs, many, offset_ref, end_ref, moved_ref, *rest):
    packed_refs = rest[: 2 * many]
    keep_ref, high_ref, both_ref, flip_ref, put_ref, out_ref, spectrum = rest[2 * many :]
    columns = high_ref.shape[1]
    left = lax.broadcasted_iota(jnp.int32, (GROUP, LANES), 1) < 2 * WAVES
    end = lax.broadcasted_iota(jnp.int32, (GROUP, LANES), 0) < GROUP * end_ref[0]
    blocks = columns // (2 * WAVES)

    def unpack(arrived_ref, held_ref):
        def load(block, group):
            at = jnp.minimum(offset_ref[block] + group, cap - 1)
            return jnp.where(end, arrived_ref[at, 0], held_ref[at, 0])

        for group in range(FROWS // GROUP):
            for pair in range((blocks + 1) // 2):
                even = load(2 * pair, group)
                odd = load(2 * pair + 1, group) if 2 * pair + 1 < blocks else even
                where = slice(GROUP * group, GROUP * (group + 1)), slice(LANES * pair, LANES * (pair + 1))
                keep = keep_ref[where]
                a = jnp.where(left, even, pltpu.roll(odd, 2 * WAVES, 1))
                b = jnp.where(left, pltpu.roll(even, 2 * WAVES, 1), odd)
                spectrum[(0,) + where] = jnp.where(keep != 0.0, a * keep, 0.0)
                spectrum[(1,) + where] = jnp.where(keep != 0.0, b * keep, 0.0)

    if many == 1:
        unpack(*packed_refs)
    else:
        for index in range(many):
            pl.when(pl.program_id(0) // pairs == index)(
                functools.partial(unpack, packed_refs[2 * index], packed_refs[2 * index + 1])
            )
    length = high_ref.shape[0]
    s_high, s_low = halves(spectrum[...].reshape(2 * FROWS, -1)[:, :columns])
    last = ((1,), (1,))
    with_high = mxu(both_ref[...], s_high, last)
    back = with_high[:length] + with_high[length:] + mxu(high_ref[...], s_low, last)
    for s in range(2):
        pieces = jnp.concatenate(halves(back[:, s * FROWS : (s + 1) * FROWS] * flip_ref[...]), axis=1)
        out_ref[s] = moved_ref[s] + mxu(pieces, put_ref[...])


RESIDENT = pl.BlockSpec(memory_space=pltpu.VMEM)


def forward(base, size, cap, offsets, regions, tracer, edges, weights, source, stays, pick, sign, high, low, out):
    tags, length, lats = tracer.shape
    pairs = size // 2
    constants = [weights, source, stays, pick, sign, high, low]
    specs = [
        pl.BlockSpec((2, length, lats), lambda p, *_: (base // 2 + p, 0, 0)),
        pl.BlockSpec((2, 4, lats), lambda p, *_: (base // 2 + p, 0, 0)),
    ] + [RESIDENT] * len(constants)
    operands = [offsets, regions, tracer, edges] + constants
    aliases = {}
    if out is not None:
        specs.append(pl.BlockSpec(memory_space=pl.ANY))
        operands.append(out)
        aliases = {len(operands) - 1: 0}
    grid_spec = pltpu.PrefetchScalarGridSpec(
        num_scalar_prefetch=2,
        grid=(pairs,),
        in_specs=specs,
        out_specs=[
            pl.BlockSpec((2, length, lats), lambda p, *_: (base // 2 + p, 0, 0)),
            pl.BlockSpec((cap, 1, GROUP, LANES), lambda p, *_: (0, p, 0, 0)),
        ],
        scratch_shapes=[
            pltpu.VMEM((2, 64, lats), jnp.float32),
            pltpu.VMEM((4 * (-(-length // 16) * 16), lats), jnp.bfloat16),
            pltpu.VMEM((2 * FROWS, -(-high.shape[1] // LANES) * LANES), jnp.float32),
        ],
    )
    flops = size * 2 * length * (2 * lats * FROWS + 3 * high.shape[1] * FROWS)
    return pl.pallas_call(
        functools.partial(forward_kernel, cap, first=base),
        grid_spec=grid_spec,
        out_shape=[
            jax.ShapeDtypeStruct(tracer.shape, jnp.float32),
            jax.ShapeDtypeStruct((cap, pairs, GROUP, LANES), jnp.float32),
        ],
        input_output_aliases=aliases,
        compiler_params=pltpu.CompilerParams(vmem_limit_bytes=VMEM),
        cost_estimate=pl.CostEstimate(flops=flops, bytes_accessed=5 * size * length * lats * 4, transcendentals=0),
        name="step_and_transform",
    )(*operands)


def inverse(base, size, cap, offsets, end, out, packed, keep, high, both, flip, put):
    tags, length, lats = out.shape
    pairs, many = size // 2, len(packed)
    constants = [keep, high, both, flip, put]
    specs = [pl.BlockSpec((2, length, lats), lambda p, *_: (base // 2 + p, 0, 0))]
    for index in range(many):
        at = lambda p, *_, start=index * pairs: (0, jnp.clip(p - start, 0, pairs - 1), 0, 0)
        specs += [pl.BlockSpec((cap, 1, GROUP, LANES), at)] * 2
    grid_spec = pltpu.PrefetchScalarGridSpec(
        num_scalar_prefetch=2,
        grid=(many * pairs,),
        in_specs=specs + [RESIDENT] * len(constants),
        out_specs=pl.BlockSpec((2, length, lats), lambda p, *_: (base // 2 + p, 0, 0)),
        scratch_shapes=[pltpu.VMEM((2, FROWS, keep.shape[1]), jnp.float32)],
    )
    flops = many * size * 2 * length * (2 * lats * FROWS + 3 * high.shape[1] * FROWS)
    return pl.pallas_call(
        functools.partial(inverse_kernel, cap, pairs, many),
        grid_spec=grid_spec,
        out_shape=jax.ShapeDtypeStruct(out.shape, jnp.float32),
        input_output_aliases={2: 0},
        compiler_params=pltpu.CompilerParams(vmem_limit_bytes=VMEM),
        cost_estimate=pl.CostEstimate(
            flops=flops, bytes_accessed=2 * many * size * length * lats * 4, transcendentals=0
        ),
        name="restore",
    )(offsets, end, out, *[array for pair in packed for array in pair], *constants)


def sum_over_lon(packed, count, place):
    middle = count // 2
    total = packed
    for hop in range(middle - 1):
        inward = [(hop, hop + 1), (count - 1 - hop, count - 2 - hop)]
        total = total + lax.ppermute(total, "lon", inward)
    total = total + lax.ppermute(total, "lon", [(middle - 1, middle), (middle, middle - 1)])
    for hop in range(middle - 2, -1, -1):
        outward = [(hop + 1, hop), (count - 2 - hop, count - 1 - hop)]
        arrived = lax.ppermute(total, "lon", outward)
        total = jnp.where((place == hop) | (place == count - 1 - hop), arrived, total)
    return total


def plain_pipeline(chunks, forward_at, inverse_at, place, count, offsets):
    out = None
    for chunk in range(chunks):
        out, packed = forward_at(chunk, out, offsets)
        total = sum_over_lon(packed, count, place)
        out = inverse_at(chunk, out, [(total, total)], offsets)
    return out


def stepped_pipeline(chunks, forward_at, inverse_at, place, count, offsets):
    swap = [(0, 1), (1, 0), (2, 3), (3, 2)]
    cross = [(1, 2), (2, 1)]
    end = (place == 0) | (place == count - 1)
    own, back = {}, {}
    out, own[0] = forward_at(0, None, offsets)
    pair_sum = swapped = crossed = sent = None
    done = 0
    for t in range(chunks + 3):
        if t >= 3:
            back[t - 3] = swapped, sent
        total = None if crossed is None else pair_sum + crossed
        here = own.get(t)
        if here is None:
            sent = total
        else:
            sent = here if total is None else jnp.where(end, here, total)
        pair_sum = own[t - 1] + swapped if 1 <= t <= chunks else None
        token = offsets
        if t < chunks + 2:
            sending = [x for x in (sent, pair_sum) if x is not None]
            token, out, *sending = lax.optimization_barrier((offsets, out, *sending))
            if pair_sum is not None:
                pair_sum = sending.pop()
            if sent is not None:
                sent = sending.pop()
            swapped = None if sent is None else lax.ppermute(sent, "lon", swap)
            crossed = None if pair_sum is None else lax.ppermute(pair_sum, "lon", cross)
        if t + 1 < chunks:
            out, own[t + 1] = forward_at(t + 1, out, token)
        quota = chunks if t == chunks + 2 else -(-(chunks - 1 - done) // (chunks + 2 - t)) if t >= chunks - 1 else 0
        ready = [back[i] for i in range(done, min(done + quota, chunks)) if i in back]
        if ready:
            out = inverse_at(done, out, ready, token)
            done += len(ready)
    return out


def ring_edges(first, last, count):
    forward_ring = [(i, (i + 1) % count) for i in range(count)]
    backward_ring = [((i + 1) % count, i) for i in range(count)]
    before = lax.ppermute(last, "lon", forward_ring)
    after = lax.ppermute(first, "lon", backward_ring)
    return before, after


def body(tracer, courant, thickness, emission, region_map, filter_mask, cutoff):
    tracer = tracer[:, 0]
    courant, thickness = courant[:, 0], thickness[0]
    tags, length, lats = tracer.shape
    count = lax.axis_size("lon")
    place = lax.axis_index("lon")
    full = length * count
    nyquist = full // 2
    groups = FROWS // GROUP
    backward_ring = [((i + 1) % count, i) for i in range(count)]

    flipped = cutoff > nyquist - 1 - cutoff
    reach = jnp.minimum(cutoff, nyquist - 1 - cutoff)
    masked = filter_mask == 1
    score = jnp.where(masked, reach + 2, 0)
    lat = jnp.arange(lats, dtype=jnp.int32)
    ahead = (score[None, :] > score[:, None]) | ((score[None, :] == score[:, None]) & (lat[None, :] < lat[:, None]))
    rank = jnp.sum(ahead.astype(jnp.int32), axis=1)
    chosen = rank[:, None] == jnp.arange(FROWS, dtype=jnp.int32)[None, :]
    row_reach = jnp.sum(jnp.where(chosen, reach[:, None], 0), axis=0)
    row_flipped = jnp.any(chosen & flipped[:, None], axis=0)
    one_hot = chosen.astype(jnp.bfloat16)
    put = one_hot.T

    blocks = nyquist // 2 // WAVES
    starts = jnp.arange(blocks, dtype=jnp.int32) * WAVES
    needed = jnp.sum((row_reach[None, :] >= starts[:, None]).astype(jnp.int32), axis=1)
    taken = (needed + GROUP - 1) // GROUP
    offsets = jnp.sum(
        jnp.where(jnp.arange(blocks)[None, :] < jnp.arange(blocks)[:, None], taken[None, :], 0), axis=1
    ).astype(jnp.int32)
    used = jnp.sum(taken)

    lane = jnp.arange(-(-blocks * 2 * WAVES // LANES) * LANES, dtype=jnp.int32)
    wave = lane // (2 * WAVES) * WAVES + lane % WAVES
    scaling = jnp.where(wave == 0, 1.0 / full, 2.0 / full).astype(jnp.float32)
    keep = jnp.where(wave[None, :] <= row_reach[:, None], scaling[None, :], 0.0)
    high, low = (
        lax.dynamic_slice_in_dim(jnp.asarray(table), place * length, length, 0) for table in wave_table(full)
    )
    odd = (place * length + jnp.arange(length, dtype=jnp.int32)) % 2 == 1
    sign = jnp.where(odd[:, None] & row_flipped[None, :], -1.0, 1.0).astype(jnp.float32)
    flip = jnp.where(row_flipped[None, :], -sign, sign)
    stays = jnp.where(masked & ~flipped, 0.0, 1.0).astype(jnp.float32)[None, :]

    largest = blocks * groups
    both = jnp.concatenate([high, low])
    put = jnp.concatenate([put, put])
    is_end = ((place == 0) | (place == count - 1)).astype(jnp.int32).reshape(1)
    sizes = [CHUNK] * (tags // CHUNK)
    bases = [sum(sizes[:i]) for i in range(len(sizes))]

    tag_count, tag = lax.axis_size("tag"), lax.axis_index("tag")
    if tag_count == 2:
        cross = [(0, 1), (1, 0)]
        other, other_thick = lax.ppermute(courant, "tag", cross), lax.ppermute(thickness, "tag", cross)
        ahead_zonal = courant[0, :1]
        same = lax.ppermute(ahead_zonal, "lon", backward_ring)
        skew = lax.ppermute(ahead_zonal, ("lon", "tag"), [((i + 1) % count * 2, i * 2 + 1) for i in range(count)])
        zonal_end = jnp.where(tag == 0, same, skew)

        def in_order(mine, theirs, axis):
            return jnp.concatenate([jnp.where(tag == 0, mine, theirs), jnp.where(tag == 0, theirs, mine)], axis=axis)

        gathered, thick = in_order(courant, other, 1), in_order(thickness, other_thick, 0)
    else:
        gathered = lax.all_gather(courant, "tag", axis=1, tiled=True)
        thick = lax.all_gather(thickness, "tag", axis=0, tiled=True)
        zonal_end = lax.all_gather(lax.ppermute(courant[0, :1], "lon", backward_ring), "tag")[0]
    edges = jnp.concatenate(ring_edges(tracer[:, :2], tracer[:, length - 2 :], count), axis=1)

    def run(cap):
        weights, keep_, both_, flip_, put_, edges_ = lax.optimization_barrier((stencil_weights(gathered, thick, zonal_end), keep, both, flip, put, edges))

        def forward_at(chunk, out, offsets):
            return forward(
                bases[chunk], sizes[chunk], cap, offsets, region_map, tracer, edges_, weights, emission, stays, one_hot,
                sign, high, low, out,
            )

        def inverse_at(chunk, out, packed, offsets):
            return inverse(bases[chunk], CHUNK, cap, offsets, is_end, out, packed, keep_, high, both_, flip_, put_)

        pipeline = stepped_pipeline if count == 4 else plain_pipeline
        return pipeline(len(sizes), forward_at, inverse_at, place, count, offsets)

    caps = [int(share * largest) + 1 for share in CAPS]
    if len(caps) == 1:
        out = run(caps[0])
    else:
        index = sum((used >= cap).astype(jnp.int32) for cap in caps[:-1])
        out = lax.switch(index, [functools.partial(run, cap) for cap in caps])
    return out[:, None]


def solution(mesh):
    in_specs = (
        P(("runs", "tag"), "lev", "lon", None),
        P(None, ("runs", "lev"), ("lon", "tag"), None),
        P(("runs", "lev"), ("lon", "tag"), None),
        P(None, "lon", None),
        P(("runs", "tag")),
        P(),
        P(),
    )
    out_specs = P(("runs", "tag"), "lev", "lon", None)
    return jax.shard_map(body, mesh=mesh, in_specs=in_specs, out_specs=out_specs, check_vma=False)
```
